512 devices in a mesh: subj: 16 (over x, z_hi, core), patch: 32 (over y, z_lo).
Axes of the slice: x: 4, y: 4, z: 16 (z_hi: 2, z_lo: 8; z = z_hi * 8 + z_lo), core: 2. Of those that a mesh axis runs over, the one named last changes fastest.
Arguments:
- tokens: bfloat16 [16, 256, 128, 512], P('subj', 'patch'), may hold values from -40 to 40
- patch_ids: int32 [256], P('patch'), may hold values from 0 to 255, each once
- patch_embed: bfloat16 [256, 512], replicated, may hold values from -6 to 6
- scene_ids: int32 [128], replicated, may hold values from 0 to 31, never falling along the last dimension, each value on 1 to 8 neighbouring positions
- norm_one: float32 [512], replicated, may hold values from 0.1 to 1.9
- query_one: bfloat16 [512, 256], replicated, may hold values from -0.25 to 0.25
- key_one: bfloat16 [512, 256], replicated, may hold values from -0.25 to 0.25
- value_one: bfloat16 [512, 256], replicated, may hold values from -0.25 to 0.25
- key_gain_one: float32 [256], replicated, may hold values from 0.5 to 200
- out_one: bfloat16 [256, 512], replicated, may hold values from -0.75 to 0.75
- norm_two: float32 [512], replicated, may hold values from 0.1 to 1.9
- query_two: bfloat16 [512, 256], replicated, may hold values from -0.25 to 0.25
- key_two: bfloat16 [512, 256], replicated, may hold values from -0.25 to 0.25
- value_two: bfloat16 [512, 256], replicated, may hold values from -0.25 to 0.25
- key_gain_two: float32 [256], replicated, may hold values from 0.5 to 200
- out_two: bfloat16 [256, 512], replicated, may hold values from -0.375 to 0.375
Outputs:
- layer_out: float32 [16, 256, 128, 512], P('subj', 'patch')
The draws below stay inside these ranges and needn't reach their ends.
Inputs may be any that keep to these rules, and one draw needn't show every extreme that they name: `patch_ids`: every patch of the table appears in exactly one slot. `scene_ids`: never falls along the frames; each scene lasts 1 to 8 frames.
All inputs are finite; a program needn't handle non-finite values.
Results may differ from the reference program's by a relative error of at most 0.018.
The reference program's roundings to bfloat16 on the way count: a program that leaves them out, or rounds other values in their place, can miss the bound.
Values may be sent and summed in bfloat16 or wider, within the bound.
A program may use at most 64 MiB of HBM per device.

```python
import math
import jax
import jax.numpy as jnp
import numpy as np
from jax import lax

D = 512
HEADS = 4
HEAD_DIM = 64
RADIUS = 2
SUBJECTS = 16
PATCHES = 256
FRAMES = 128


def draw_tokens(key, part):
    full_shape = (SUBJECTS, PATCHES, FRAMES, D)
    key_noise, key_rows, key_cols = jax.random.split(jax.random.fold_in(key, 3), 3)
    noise_draw = jnp.clip(jax.random.normal(key_noise, full_shape, jnp.float32), -4.0, 4.0)
    row_scale = jnp.exp(jax.random.uniform(key_rows, (SUBJECTS, PATCHES, FRAMES, 1), jnp.float32, math.log(0.3), math.log(3.0)))
    column_scale = jnp.exp(jax.random.uniform(key_cols, (D,), jnp.float32, math.log(0.3), math.log(3.0)))
    drawn = noise_draw * row_scale * column_scale
    return drawn.astype(jnp.bfloat16)


def head_gains(key):
    key_rank, key_channel = jax.random.split(key)
    head_rank = jax.random.permutation(key_rank, HEADS).astype(jnp.float32) / (HEADS - 1)
    channel_gain = jnp.exp(jax.random.uniform(key_channel, (HEADS, HEAD_DIM), jnp.float32, math.log(0.8), math.log(1.25)))
    head_scale = 1.5 * jnp.exp(head_rank * math.log(4.0))
    return (head_scale[:, None] * channel_gain).reshape(HEADS * HEAD_DIM)


def draw_key_gain_one(key, part):
    return head_gains(jax.random.fold_in(key, 11))


def draw_key_gain_two(key, part):
    return head_gains(jax.random.fold_in(key, 12))


def profile(count, total, limit, skew):
    weights = [(1 << 20) // math.isqrt(rank ** skew) + 1 for rank in range(2, count + 1)]
    rest, holding = total - limit - (count - 1), [1] * (count - 1)
    while rest > 0:
        candidates = [i for i in range(count - 1) if holding[i] < limit]
        pool, remaining = sum([weights[i] for i in candidates]), rest
        for i in candidates:
            addition = min(limit - holding[i], max(1, remaining * weights[i] // pool), rest)
            holding[i] = holding[i] + addition
            rest = rest - addition
    return np.array([limit] + holding)


def uneven_parts(rng, count, total, bound, lean):
    if count == 2:
        one = jax.random.randint(rng, (), max(1, total - bound), min(bound, total - 1) + 1)
        return jnp.stack([one, total - one])
    lengths = jnp.asarray(profile(count, total, bound, lean), jnp.int32)
    twos = (count - 1) // 2
    donor, sink = lengths[1:1 + 2 * twos:2], lengths[2:2 + 2 * twos:2]
    margin = jnp.minimum(donor - 1, bound - sink)
    shifted = jax.random.randint(jax.random.fold_in(rng, 1), (twos,), 0, 1 << 20) % (margin + 1)
    lengths = lengths.at[1:1 + 2 * twos:2].set(donor - shifted).at[2:2 + 2 * twos:2].set(sink + shifted)
    return lengths[jax.random.permutation(jax.random.fold_in(rng, 2), count)]


def normal_values(own_key, extent, deviation, bound, kind=jnp.bfloat16):
    values = deviation * jax.random.normal(own_key, extent, jnp.float32)
    return jnp.clip(values, min=-bound, max=bound).astype(kind)


def setup_inputs(seed: int = 0) -> dict:
    streams_of = jax.random.split(jax.random.key(seed), 17)
    tokens = draw_tokens(jax.random.fold_in(streams_of[16], 71), 0)
    patch_ids = jax.random.permutation(streams_of[1], PATCHES).astype(jnp.int32)
    patch_embed = normal_values(streams_of[2], (PATCHES, D), 1.0, 6.0)
    scene_ids = jnp.searchsorted(jnp.cumsum(uneven_parts(streams_of[3], FRAMES // 4, FRAMES, 8, 0)), jnp.arange(FRAMES), side="right").astype(jnp.int32)
    norm_one = jnp.clip(1.0 + 0.18 * jax.random.normal(streams_of[4], (D,), jnp.float32), 0.1, 1.9)
    query_one = normal_values(streams_of[5], (D, HEADS * HEAD_DIM), D ** -0.5, 0.25)
    key_one = normal_values(streams_of[6], (D, HEADS * HEAD_DIM), D ** -0.5, 0.25)
    value_one = normal_values(streams_of[7], (D, HEADS * HEAD_DIM), D ** -0.5, 0.25)
    key_gain_one = draw_key_gain_one(jax.random.fold_in(streams_of[16], 71), 0)
    out_one = normal_values(streams_of[9], (HEADS * HEAD_DIM, D), (HEADS * HEAD_DIM // 4) ** -0.5, 0.75)
    norm_two = jnp.clip(1.0 + 0.18 * jax.random.normal(streams_of[10], (D,), jnp.float32), 0.1, 1.9)
    query_two = normal_values(streams_of[11], (D, HEADS * HEAD_DIM), D ** -0.5, 0.25)
    key_two = normal_values(streams_of[12], (D, HEADS * HEAD_DIM), D ** -0.5, 0.25)
    value_two = normal_values(streams_of[13], (D, HEADS * HEAD_DIM), D ** -0.5, 0.25)
    key_gain_two = draw_key_gain_two(jax.random.fold_in(streams_of[16], 71), 0)
    out_two = normal_values(streams_of[15], (HEADS * HEAD_DIM, D), (HEADS * HEAD_DIM) ** -0.5, 0.375)
    return {"tokens": tokens, "patch_ids": patch_ids, "patch_embed": patch_embed, "scene_ids": scene_ids, "norm_one": norm_one, "query_one": query_one, "key_one": key_one, "value_one": value_one, "key_gain_one": key_gain_one, "out_one": out_one, "norm_two": norm_two, "query_two": query_two, "key_two": key_two, "value_two": value_two, "key_gain_two": key_gain_two, "out_two": out_two}


norm_epsilon = 1e-05

def rms_scale(features, scale_row):
    mean_square = lax.optimization_barrier(jnp.mean(features * features, axis=-1, keepdims=True))
    return features * lax.rsqrt(mean_square + norm_epsilon) * scale_row

def project(flat_rows, weight):
    return jnp.dot(flat_rows, weight, preferred_element_type=jnp.float32)

def softmax_over(scores, axes):
    highest = lax.optimization_barrier(jnp.max(scores, axis=axes, keepdims=True))
    raised = jnp.exp(scores - highest)
    return raised / lax.optimization_barrier(jnp.sum(raised, axis=axes, keepdims=True))

def reference(tokens, patch_ids, patch_embed, scene_ids, norm_one, query_one, key_one, value_one, key_gain_one, out_one, norm_two, query_two, key_two, value_two, key_gain_two, out_two):
    inner_width = HEADS * HEAD_DIM
    score_scale = 1.0 / math.sqrt(HEAD_DIM)
    key_span = 2 * RADIUS + 1
    embedded = jnp.take(patch_embed, patch_ids.astype(jnp.int32), axis=0).astype(jnp.float32)
    rim_ids = jnp.full((RADIUS,), -1, jnp.int32)
    scene_pad = jnp.concatenate([rim_ids, scene_ids.astype(jnp.int32), rim_ids])

    def section_one(subject_tokens):
        residual = subject_tokens.astype(jnp.float32) + embedded[:, None, :]
        normed = rms_scale(residual, norm_one).astype(jnp.bfloat16).reshape(PATCHES * FRAMES, D)
        query_heads = project(normed, query_one).astype(jnp.bfloat16).reshape(PATCHES, FRAMES, HEADS, HEAD_DIM)
        key_heads = (project(normed, key_one) * key_gain_one).astype(jnp.bfloat16).reshape(PATCHES, FRAMES, HEADS, HEAD_DIM)
        value_heads = project(normed, value_one).astype(jnp.bfloat16).reshape(PATCHES, FRAMES, HEADS, HEAD_DIM)
        padding = ((0, 0), (RADIUS, RADIUS), (0, 0), (0, 0))
        key_heads = jnp.pad(key_heads, padding)
        value_heads = jnp.pad(value_heads, padding)

        def one_frame(frame_index):
            query_now = lax.dynamic_index_in_dim(query_heads, frame_index, 1, keepdims=False).astype(jnp.float32)
            key_near = lax.dynamic_slice_in_dim(key_heads, frame_index, key_span, 1).astype(jnp.float32)
            value_near = lax.dynamic_slice_in_dim(value_heads, frame_index, key_span, 1).astype(jnp.float32)
            scene_near = lax.dynamic_slice_in_dim(scene_pad, frame_index, key_span)
            usable = scene_near == scene_near[RADIUS]
            scores = jnp.einsum('ihd,jehd->hiej', query_now, key_near) * score_scale
            scores = jnp.where(usable[None, None, :, None], scores, -jnp.inf)
            weights = softmax_over(scores, (2, 3)).astype(jnp.bfloat16)
            mixed_rows = jnp.einsum('hiej,jehd->ihd', weights.astype(jnp.float32), value_near)
            return mixed_rows.astype(jnp.bfloat16).reshape(PATCHES, inner_width)
        mixed_all = lax.map(one_frame, jnp.arange(FRAMES, dtype=jnp.int32))
        mixed_all = jnp.transpose(mixed_all, (1, 0, 2)).reshape(PATCHES * FRAMES, inner_width)
        return residual + project(mixed_all, out_one).reshape(PATCHES, FRAMES, D)
    after_one = lax.map(section_one, tokens)

    def project_two(subject_rows):
        normed = rms_scale(subject_rows, norm_two).astype(jnp.bfloat16).reshape(PATCHES * FRAMES, D)
        query_rows = project(normed, query_two).astype(jnp.bfloat16)
        key_rows = (project(normed, key_two) * key_gain_two).astype(jnp.bfloat16)
        value_rows = project(normed, value_two).astype(jnp.bfloat16)
        return (query_rows, key_rows, value_rows)
    query_all, key_all, value_all = lax.map(project_two, after_one)
    token_total = PATCHES * FRAMES
    token_block = math.gcd(token_total, 512)
    block_count = token_total // token_block

    def to_blocks(stacked):
        shaped = stacked.reshape(SUBJECTS, block_count, token_block, HEADS, HEAD_DIM)
        return jnp.transpose(shaped, (1, 0, 2, 3, 4))

    def cross_block(members):
        query_block = members[0].astype(jnp.float32)
        key_block = members[1].astype(jnp.float32)
        value_block = members[2].astype(jnp.float32)
        scores = jnp.einsum('snhd,rnhd->nhsr', query_block, key_block) * score_scale
        weights = softmax_over(scores, (3,)).astype(jnp.bfloat16)
        mixed_rows = jnp.einsum('nhsr,rnhd->snhd', weights.astype(jnp.float32), value_block)
        return mixed_rows.astype(jnp.bfloat16).reshape(SUBJECTS, token_block, inner_width)
    crossed = lax.map(cross_block, (to_blocks(query_all), to_blocks(key_all), to_blocks(value_all)))
    crossed = jnp.transpose(crossed, (1, 0, 2, 3)).reshape(SUBJECTS * token_total, inner_width)
    update = project(crossed, out_two).reshape(SUBJECTS, PATCHES, FRAMES, D)
    return after_one + update
```

```python
import functools
import math

import jax
import jax.numpy as jnp
from jax import lax
from jax.experimental import pallas as pl
from jax.experimental.pallas import tpu as pltpu
from jax.sharding import PartitionSpec as P

MESH = pl.DeviceIdType.MESH
HEADS = 4
HEAD_DIM = 64
EPS = 1e-05
F32 = jnp.float32
BF16 = jnp.bfloat16
EXP_SCALE = math.log2(math.e) / math.sqrt(HEAD_DIM)


def coords():
    s = lax.axis_index("subj")
    p = lax.axis_index("patch")
    return s // 4, p // 8, ((s // 2) % 2) * 8 + p % 8, s % 2


def at(x, y, z, c):
    return ((x * 2 + z // 8) * 2 + c, y * 8 + z % 8)


def remote(src, dst, send, recv, device):
    return pltpu.make_async_remote_copy(
        src_ref=src, dst_ref=dst, send_sem=send, recv_sem=recv, device_id=device, device_id_type=MESH
    )


def pair_at(z, i):
    half = (i + 1) // 2
    sign = 2 * (i % 2) - 1
    return (z // 2 + 8 + sign * half) % 8


def rms(rows, gain):
    mean = jnp.mean(rows * rows, axis=-1, keepdims=True)
    return (rows * lax.rsqrt(mean + EPS) * gain).astype(BF16)


def dot(a, b):
    return jnp.dot(a, b, preferred_element_type=F32)


def dot_t(a, b):
    return lax.dot_general(a, b, (((1,), (1,)), ((), ())), preferred_element_type=F32)


def one_hot_rows(ids, table):
    lane = lax.broadcasted_iota(jnp.int32, ids.shape, 1)
    low = jnp.where(ids == lane, 1.0, 0.0).astype(F32)
    high = jnp.where(ids == lane + 128, 1.0, 0.0).astype(F32)
    picked = jnp.concatenate([low, high], axis=1).astype(BF16)
    return dot(picked, table)


def spread_kernel(
    tok, ids, table, gain, wq, wk, wv, key_gain,
    q_all, kv_all, tok2, emb,
    land, ids_land, q_out, kv_out,
    tok_s, tok_r, ids_s, ids_r, q_s, q_r, kv_s, kv_r, own_s, edge_s, edge_r,
):
    x, y, z, c = coords()
    zh, zl = z // 8, z % 8
    barrier = pltpu.get_barrier_semaphore()
    for d in range(1, 16):
        pl.semaphore_signal(barrier, inc=1, device_id=at(x, y, (z + d) % 16, c), device_id_type=MESH)
    for d in range(1, 4):
        pl.semaphore_signal(barrier, inc=1, device_id=at(x, (y + d) % 4, z, c), device_id_type=MESH)
    pl.semaphore_wait(barrier, 18)

    def tok_copy(t):
        return remote(tok.at[t], land.at[z], tok_s.at[t], tok_r.at[z], at(x, y, t, c))

    def tok_wait(s):
        remote(tok.at[s], land.at[s], tok_s.at[s], tok_r.at[s], at(x, y, s, c)).wait_recv()

    other = z + 1 - 2 * (z % 2)
    for d in range(1, 8):
        t = zh * 8 + (zl + d) % 8
        remote(ids, ids_land.at[zl], ids_s.at[t % 8], ids_r.at[zl], at(x, y, t, c)).start()
    tok_copy(other).start()

    def send_pair(i, carry):
        j = pair_at(z, i)
        tok_copy(2 * j).start()
        tok_copy(2 * j + 1).start()
        return carry

    lax.fori_loop(1, 8, send_pair, 0)
    land[z] = tok[z]
    ids_land[zl] = ids[...]
    for d in range(1, 8):
        s = (zl + d) % 8
        remote(ids, ids_land.at[s], ids_s.at[s], ids_r.at[s], at(x, y, zh * 8 + s, c)).wait()
    emb[...] = one_hot_rows(ids_land[...].reshape(64, 128), table[...])

    low = lax.broadcasted_iota(jnp.int32, (128, 128), 1) < HEAD_DIM

    def own_copies(j):
        return (
            pltpu.make_async_copy(q_out.at[y, j], q_all.at[y, j], own_s.at[0, j]),
            pltpu.make_async_copy(kv_out.at[y, j], kv_all.at[y, j, pl.ds(2, 8)], own_s.at[1, j]),
        )

    def process(j):
        even = land[2 * j].astype(F32)
        odd = land[2 * j + 1].astype(F32)
        parts = []
        for f in range(8):
            parts += [even[8 * f : 8 * f + 8], odd[8 * f : 8 * f + 8]]
        rows = jnp.concatenate(parts, axis=0)
        tok2[:, j] = rows.astype(BF16).reshape(8, 16, 512)
        here = emb[pl.ds(pl.multiple_of((j % 4) * 16, 16), 16), :]
        rows = (rows.reshape(8, 16, 512) + here[None]).reshape(128, 512)
        normed = rms(rows, gain[...])
        query = dot(normed, wq[...])
        key = dot(normed, wk[...]) * key_gain[...]
        value = dot(normed, wv[...])
        for hp in range(2):
            lanes = slice(128 * hp, 128 * hp + 128)
            qp, kp, vp = query[:, lanes], key[:, lanes], value[:, lanes]
            q0 = jnp.where(low, qp, 0.0)
            q1 = jnp.where(low, pltpu.roll(qp, 64, 1), 0.0)
            kv0 = jnp.where(low, kp, pltpu.roll(vp, 64, 1))
            kv1 = jnp.where(low, pltpu.roll(kp, 64, 1), vp)
            q_out[2 * hp, j] = q0.astype(BF16).reshape(8, 16, 128)
            q_out[2 * hp + 1, j] = q1.astype(BF16).reshape(8, 16, 128)
            kv_out[2 * hp, j] = kv0.astype(BF16).reshape(8, 16, 128)
            kv_out[2 * hp + 1, j] = kv1.astype(BF16).reshape(8, 16, 128)
        for d in (1, 3, 2):
            h = (y + d) % 4
            remote(
                kv_out.at[h, j], kv_all.at[y, j, pl.ds(2, 8)], kv_s.at[h, j], kv_r.at[y, j], at(x, h, z, c)
            ).start()
            remote(q_out.at[h, j], q_all.at[y, j], q_s.at[h, j], q_r.at[y, j], at(x, h, z, c)).start()
        for copy in own_copies(j):
            copy.start()

    tok_wait(other)
    process(z // 2)

    def step(i, carry):
        j = pair_at(z, i)
        tok_wait(2 * j)
        tok_wait(2 * j + 1)
        process(j)
        return carry

    lax.fori_loop(1, 8, step, 0)

    def finish(j, carry):
        for d in range(1, 4):
            h = (y + d) % 4
            remote(
                kv_out.at[h, j], kv_all.at[h, j, pl.ds(2, 8)], kv_s.at[h, j], kv_r.at[h, j], at(x, h, z, c)
            ).wait()
            remote(q_out.at[h, j], q_all.at[h, j], q_s.at[h, j], q_r.at[h, j], at(x, h, z, c)).wait()
        for copy in own_copies(j):
            copy.wait()
        return carry

    lax.fori_loop(0, 8, finish, 0)
    down = remote(
        kv_all.at[:, :, pl.ds(2, 2)], kv_all.at[:, :, pl.ds(10, 2)],
        edge_s.at[0], edge_r.at[0], at(x, y, (z + 15) % 16, c),
    )
    up = remote(
        kv_all.at[:, :, pl.ds(8, 2)], kv_all.at[:, :, pl.ds(0, 2)],
        edge_s.at[1], edge_r.at[1], at(x, y, (z + 1) % 16, c),
    )
    down.start()
    up.start()

    def tok_done(d, carry):
        tok_copy((z + d) % 16).wait_send()
        return carry

    lax.fori_loop(1, 16, tok_done, 0)
    down.wait()
    up.wait()


def frame_kernel(scene, where_z, q_all, kv_all, mixed):
    low = lax.broadcasted_iota(jnp.int32, (256, 128), 1) < HEAD_DIM

    def frame(f, carry):
        t = where_z[0] * 8 + f
        here = scene[t]

        def same(u):
            inside = jnp.logical_and(u >= 0, u < 128)
            return jnp.where(jnp.logical_and(inside, scene[jnp.clip(u, 0, 127)] == here), 1, 0)

        before = same(t - 1)
        before2 = before * same(t - 2)
        after = same(t + 1)
        after2 = after * same(t + 2)
        start = f + 2 - before - before2
        count = 1 + before + before2 + after + after2

        def attend(n):
            outs = []
            for zh in range(2):
                pairs = slice(4 * zh, 4 * zh + 4)
                query = q_all[:, pairs, f].reshape(256, 128)
                keys = kv_all[:, pairs, pl.ds(start, n)].reshape(256 * n, 128)
                scores = dot_t(query, keys)
                top = jnp.max(scores, axis=1, keepdims=True)
                raised = jnp.exp2((scores - top) * EXP_SCALE)
                total = jnp.sum(raised, axis=1, keepdims=True)
                outs.append(dot(raised.astype(BF16), keys) / total)
            both = jnp.where(low, pltpu.roll(outs[0], 64, 1), outs[1])
            mixed[:, f] = both.astype(BF16).reshape(4, 4, 16, 128)

        for n in range(1, 6):
            pl.when(count == n)(functools.partial(attend, n))
        return carry

    lax.fori_loop(0, 8, frame, 0)


def cross_kernel(
    mixed, tok2, emb, out_one, gain, wq, wk, wv, key_gain,
    back_a, back_b,
    heads, za, zb, normed, group, q2, k2, v2, crossed, returned,
    h_s, h_r, n_s, n_r, x_s, x_r, a_s, a_r, b_s, b_r, own_s,
):
    x, y, z, c = coords()
    me = x * 2 + c
    barrier = pltpu.get_barrier_semaphore()
    for d in range(1, 16):
        pl.semaphore_signal(barrier, inc=1, device_id=at(x, y, (z + d) % 16, c), device_id_type=MESH)
    for d in range(1, 4):
        pl.semaphore_signal(barrier, inc=1, device_id=at(x, (y + d) % 4, z, c), device_id_type=MESH)
    for d in range(1, 8):
        t = (me + d) % 8
        pl.semaphore_signal(barrier, inc=1, device_id=at(t // 2, y, z, t % 2), device_id_type=MESH)
    pl.semaphore_wait(barrier, 25)

    def heads_own(k):
        frames = pl.ds(2 * k, 2)
        return pltpu.make_async_copy(mixed.at[y, frames], heads.at[y, frames], own_s.at[k])

    def send_heads(i, carry):
        k = (x + 1 + i) % 4
        frames = pl.ds(2 * k, 2)
        for d in (1, 3, 2):
            t = (y + d) % 4
            remote(
                mixed.at[t, frames], heads.at[y, frames], h_s.at[t, k], h_r.at[y, k], at(x, t, z, c)
            ).start()
        heads_own(k).start()
        return carry

    lax.fori_loop(0, 4, send_heads, 0)
    low = lax.broadcasted_iota(jnp.int32, (64, 128), 1) < HEAD_DIM

    def normed_copy(f):
        return remote(normed.at[f], group.at[me], n_s.at[f], n_r.at[me], at(f // 2, y, z, f % 2))

    def project(k):
        frames = pl.ds(2 * k, 2)
        for d in range(1, 4):
            t = (y + d) % 4
            remote(
                mixed.at[t, frames], heads.at[t, frames], h_s.at[t, k], h_r.at[t, k], at(x, t, z, c)
            ).wait()
        heads_own(k).wait()
        mixes = []
        for parity in range(2):
            part = [heads[h, 2 * k + parity].reshape(64, 128).astype(F32) for h in range(HEADS)]
            for zh in range(2):
                lanes = []
                for hp in range(2):
                    first, second = part[2 * hp], part[2 * hp + 1]
                    if zh == 0:
                        lanes.append(jnp.where(low, first, pltpu.roll(second, 64, 1)))
                    else:
                        lanes.append(jnp.where(low, pltpu.roll(first, 64, 1), second))
                mixes.append(jnp.concatenate(lanes, axis=1))
        for zh in range(2):
            for zl in range(8):
                rows = slice(8 * zl, 8 * zl + 8)
                two = jnp.concatenate([mixes[zh][rows], mixes[2 + zh][rows]], axis=0)
                za[8 * zh + zl, k] = two.astype(BF16)
        rows = jnp.concatenate(mixes, axis=0).astype(BF16)
        update = dot(rows, out_one[...])
        residual = tok2[frames].astype(F32).reshape(4, 64, 512) + emb[...][None]
        after = residual.reshape(256, 512) + update
        normed[frames] = rms(after, gain[...]).reshape(2, 2, 64, 512)

    def step(i, carry):
        k = (x + 1 + i) % 4
        project(k)
        normed_copy(2 * k).start()
        normed_copy(2 * k + 1).start()
        return carry

    lax.fori_loop(0, 3, step, 0)
    project(x)
    partner = 2 * x + 1 - c
    normed_copy(partner).start()

    def a_copy(t):
        return remote(za.at[t], back_a.at[z], a_s.at[t], a_r.at[z], at(x, y, t, c))

    def b_copy(t):
        return remote(zb.at[t], back_b.at[z], b_s.at[t], b_r.at[z], at(x, y, t, c))

    other = z + 1 - 2 * (z % 2)
    a_copy(other).start()

    def send_a(i, carry):
        j = pair_at(z, i)
        a_copy(2 * j).start()
        a_copy(2 * j + 1).start()
        return carry

    lax.fori_loop(1, 8, send_a, 0)
    back_a[z] = za[z]
    group[me] = normed[me]

    def qkv(s):
        rows = group[s].reshape(128, 512)
        query = dot(rows, wq[...]).astype(BF16).reshape(2, 4, 16, 256)
        key = (dot(rows, wk[...]) * key_gain[...]).astype(BF16).reshape(2, 4, 16, 256)
        value = dot(rows, wv[...]).astype(BF16).reshape(2, 4, 16, 256)
        for zh in range(2):
            q2[:, 2 * s + zh] = query[zh]
            k2[:, 2 * s + zh] = key[zh]
            v2[:, 2 * s + zh] = value[zh]

    qkv(me)

    def qkv_step(i, carry):
        s = (me + i) % 8
        remote(normed.at[s], group.at[s], n_s.at[s], n_r.at[s], at(s // 2, y, z, s % 2)).wait()
        qkv(s)
        return carry

    lax.fori_loop(1, 8, qkv_step, 0)
    row = lax.broadcasted_iota(jnp.int32, (256, 256), 0) % 16
    column = lax.broadcasted_iota(jnp.int32, (256, 256), 1)
    alike = row == column % 16
    head_of = column // HEAD_DIM

    def cross(g, carry):
        query = q2[g].reshape(256, 256)
        key = k2[g].reshape(256, 256)
        value = v2[g].reshape(256, 256)
        result = jnp.zeros((256, 256), F32)
        for h in range(HEADS):
            mine = head_of == h
            one = jnp.where(mine, query.astype(F32), 0.0).astype(BF16)
            scores = jnp.where(alike, dot_t(one, key), -jnp.inf)
            top = jnp.max(scores, axis=1, keepdims=True)
            raised = jnp.exp2((scores - top) * EXP_SCALE)
            total = jnp.sum(raised, axis=1, keepdims=True)
            result = jnp.where(mine, dot(raised.astype(BF16), value) / total, result)
        result = result.astype(BF16).reshape(8, 2, 16, 256)
        crossed[:, g] = result[:, 0]
        crossed[:, 4 + g] = result[:, 1]
        return carry

    lax.fori_loop(0, 4, cross, 0)

    def crossed_copy(s):
        return remote(crossed.at[s], returned.at[me], x_s.at[s], x_r.at[me], at(s // 2, y, z, s % 2))

    def send_crossed(i, carry):
        crossed_copy((me + i) % 8).start()
        return carry

    lax.fori_loop(1, 8, send_crossed, 0)
    returned[me] = crossed[me]

    def wait_crossed(i, carry):
        s = (me + i) % 8
        remote(crossed.at[s], returned.at[s], x_s.at[s], x_r.at[s], at(s // 2, y, z, s % 2)).wait()
        return carry

    lax.fori_loop(1, 8, wait_crossed, 0)

    def regroup(j):
        block = returned[:, j].astype(F32)
        for parity in range(2):
            rows = slice(8 * parity, 8 * parity + 8)
            whole = jnp.concatenate([block[f, rows] for f in range(8)], axis=0)
            zb[2 * j + parity] = whole.astype(BF16).reshape(4, 16, 256)

    regroup(z // 2)
    b_copy(other).start()

    def send_b(i, carry):
        j = pair_at(z, i)
        regroup(j)
        b_copy(2 * j).start()
        b_copy(2 * j + 1).start()
        return carry

    lax.fori_loop(1, 8, send_b, 0)
    back_b[z] = zb[z]

    def finish(d, carry):
        s = (z + d) % 16
        remote(za.at[s], back_a.at[s], a_s.at[s], a_r.at[s], at(x, y, s, c)).wait()
        remote(zb.at[s], back_b.at[s], b_s.at[s], b_r.at[s], at(x, y, s, c)).wait()
        return carry

    lax.fori_loop(1, 16, finish, 0)


def final_kernel(tok, ids, table, back_a, back_b, out_one, out_two, out):
    emb = one_hot_rows(ids[...], table[...])

    def step(i, carry):
        four = pl.ds(4 * i, 4)
        rows = tok[four].astype(F32).reshape(32, 8, 512) + emb[None]
        mixed_a = back_a[four].reshape(256, 256)
        mixed_b = back_b[four].reshape(256, 256)
        whole = rows.reshape(256, 512) + dot(mixed_a, out_one[...]) + dot(mixed_b, out_two[...])
        turned = jnp.transpose(whole.reshape(32, 8, 512), (1, 0, 2))
        out[:, pl.ds(pl.multiple_of(i * 32, 32), 32), :] = turned
        return carry

    lax.fori_loop(0, 4, step, 0)


VMEM = pl.BlockSpec(memory_space=pltpu.VMEM)
SMEM = pl.BlockSpec(memory_space=pltpu.SMEM)
DMA = pltpu.SemaphoreType.DMA


def shape(*dims, dtype=BF16):
    return jax.ShapeDtypeStruct(dims, dtype)


def params(**more):
    return pltpu.CompilerParams(vmem_limit_bytes=40 << 20, **more)


def on_device(
    tokens, patch_ids, patch_embed, scene_ids,
    norm_one, query_one, key_one, value_one, key_gain_one, out_one,
    norm_two, query_two, key_two, value_two, key_gain_two, out_two,
):
    tok = jnp.transpose(tokens.reshape(8, 16, 8, 512), (1, 2, 0, 3)).reshape(16, 64, 512)
    ids = jnp.broadcast_to(patch_ids[:, None], (8, 128))
    q_all, kv_all, tok2, emb = pl.pallas_call(
        spread_kernel,
        out_shape=(
            shape(4, 8, 8, 16, 128),
            shape(4, 8, 12, 16, 128),
            shape(8, 8, 16, 512),
            shape(64, 512, dtype=F32),
        ),
        in_specs=[VMEM] * 8,
        out_specs=(VMEM,) * 4,
        scratch_shapes=[
            pltpu.VMEM((16, 64, 512), BF16),
            pltpu.VMEM((8, 8, 128), jnp.int32),
            pltpu.VMEM((4, 8, 8, 16, 128), BF16),
            pltpu.VMEM((4, 8, 8, 16, 128), BF16),
            DMA((16,)), DMA((16,)), DMA((8,)), DMA((8,)),
            DMA((4, 8)), DMA((4, 8)), DMA((4, 8)), DMA((4, 8)), DMA((2, 8)), DMA((2,)), DMA((2,)),
        ],
        compiler_params=params(collective_id=0, has_side_effects=True),
        name="spread",
    )(tok, ids, patch_embed, norm_one[None], query_one, key_one, value_one, key_gain_one[None])
    x, y, z, c = coords()
    mixed = pl.pallas_call(
        frame_kernel,
        out_shape=shape(4, 8, 4, 16, 128),
        in_specs=[SMEM, SMEM, VMEM, VMEM],
        out_specs=VMEM,
        compiler_params=params(),
        name="frames",
    )(scene_ids, z.astype(jnp.int32)[None], q_all, kv_all)
    back_a, back_b = pl.pallas_call(
        cross_kernel,
        out_shape=(shape(16, 4, 16, 256), shape(16, 4, 16, 256)),
        in_specs=[VMEM] * 9,
        out_specs=(VMEM,) * 2,
        scratch_shapes=[
            pltpu.VMEM((4, 8, 4, 16, 128), BF16),
            pltpu.VMEM((16, 4, 16, 256), BF16),
            pltpu.VMEM((16, 4, 16, 256), BF16),
            pltpu.VMEM((8, 2, 64, 512), BF16),
            pltpu.VMEM((8, 2, 64, 512), BF16),
            pltpu.VMEM((4, 16, 16, 256), BF16),
            pltpu.VMEM((4, 16, 16, 256), BF16),
            pltpu.VMEM((4, 16, 16, 256), BF16),
            pltpu.VMEM((8, 8, 16, 256), BF16),
            pltpu.VMEM((8, 8, 16, 256), BF16),
            DMA((4, 4)), DMA((4, 4)), DMA((8,)), DMA((8,)), DMA((8,)), DMA((8,)),
            DMA((16,)), DMA((16,)), DMA((16,)), DMA((16,)), DMA((4,)),
        ],
        compiler_params=params(collective_id=1, has_side_effects=True),
        name="cross",
    )(mixed, tok2, emb, out_one, norm_two[None], query_two, key_two, value_two, key_gain_two[None])
    out = pl.pallas_call(
        final_kernel,
        out_shape=shape(8, 128, 512, dtype=F32),
        in_specs=[VMEM] * 7,
        out_specs=VMEM,
        compiler_params=params(),
        name="final",
    )(tok, ids, patch_embed, back_a, back_b, out_one, out_two)
    return out.reshape(1, 8, 128, 512)


def solution(mesh):
    return jax.shard_map(
        on_device,
        mesh=mesh,
        in_specs=(P("subj", "patch", None, None), P("patch")) + (P(),) * 14,
        out_specs=P("subj", "patch", None, None),
        check_vma=False,
    )
```

```python
import functools
import math

import jax
import jax.numpy as jnp
from jax import lax
from jax.experimental import pallas as pl
from jax.experimental.pallas import tpu as pltpu
from jax.sharding import PartitionSpec as P

MESH = pl.DeviceIdType.MESH
HEADS = 4
HEAD_DIM = 64
EPS = 1e-05
F32 = jnp.float32
BF16 = jnp.bfloat16
EXP_SCALE = math.log2(math.e) / math.sqrt(HEAD_DIM)


def coords():
    s = lax.axis_index("subj")
    p = lax.axis_index("patch")
    return s // 4, p // 8, ((s // 2) % 2) * 8 + p % 8, s % 2


def at(x, y, z, c):
    return ((x * 2 + z // 8) * 2 + c, y * 8 + z % 8)


def remote(src, dst, send, recv, device):
    return pltpu.make_async_remote_copy(
        src_ref=src, dst_ref=dst, send_sem=send, recv_sem=recv, device_id=device, device_id_type=MESH
    )


def pair_at(z, i):
    half = (i + 1) // 2
    sign = 2 * (i % 2) - 1
    return (z // 2 + 8 + sign * half) % 8


def rms(rows, gain):
    mean = jnp.mean(rows * rows, axis=-1, keepdims=True)
    return (rows * lax.rsqrt(mean + EPS) * gain).astype(BF16)


def dot(a, b):
    return jnp.dot(a, b, preferred_element_type=F32)


def dot_t(a, b):
    return lax.dot_general(a, b, (((1,), (1,)), ((), ())), preferred_element_type=F32)


def one_hot_rows(ids, table):
    lane = lax.broadcasted_iota(jnp.int32, ids.shape, 1)
    low = jnp.where(ids == lane, 1.0, 0.0).astype(F32)
    high = jnp.where(ids == lane + 128, 1.0, 0.0).astype(F32)
    picked = jnp.concatenate([low, high], axis=1).astype(BF16)
    return dot(picked, table)


def layer_kernel(
    scene, tok, ids, table, gain_one, wq1, wk1, wv1, key_gain_one, out_one, gain_two, wq2, wk2, wv2, key_gain_two,
    back_a, back_b,
    land, ids_land, emb, tok2, q_out, kv_out, q_all, kv_all, mixed, heads, za, zb, normed, group, q2, k2, v2,
    crossed, returned,
    tok_s, tok_r, ids_s, ids_r, q_s, q_r, kv_s, kv_r, own_s, edge_s, edge_r, h_s, h_r, n_s, n_r, x_s, x_r,
    a_s, a_r, b_s, b_r, turn_s,
):
    x, y, z, c = coords()
    zh, zl = z // 8, z % 8
    me = x * 2 + c
    other = z + 1 - 2 * (z % 2)
    below, above = (z + 15) % 16, (z + 1) % 16
    barrier = pltpu.get_barrier_semaphore()

    def greet(device):
        pl.semaphore_signal(barrier, inc=1, device_id=device, device_id_type=MESH)

    for d in range(1, 16):
        greet(at(x, y, (z + d) % 16, c))
    for d in range(1, 4):
        for near in (z, below, above):
            greet(at(x, (y + d) % 4, near, c))
    for d in range(1, 8):
        t = (me + d) % 8
        greet(at(t // 2, y, z, t % 2))
    pl.semaphore_wait(barrier, 31)

    def tok_copy(t):
        return remote(tok.at[t], land.at[z], tok_s.at[t], tok_r.at[z], at(x, y, t, c))

    def tok_wait(s):
        remote(tok.at[s], land.at[s], tok_s.at[s], tok_r.at[s], at(x, y, s, c)).wait_recv()

    tok_copy(other).start()
    for d in range(1, 8):
        t = zh * 8 + (zl + d) % 8
        remote(ids, ids_land.at[zl], ids_s.at[t % 8], ids_r.at[zl], at(x, y, t, c)).start()

    def send_pair(i, carry):
        j = pair_at(z, i)
        tok_copy(2 * j).start()
        tok_copy(2 * j + 1).start()
        return carry

    lax.fori_loop(1, 8, send_pair, 0)
    land[z] = tok[z]
    ids_land[zl] = ids[...]
    for d in range(1, 8):
        s = (zl + d) % 8
        remote(ids, ids_land.at[s], ids_s.at[s], ids_r.at[s], at(x, y, zh * 8 + s, c)).wait()
    emb[...] = one_hot_rows(ids_land[...].reshape(64, 128), table[...])

    low = lax.broadcasted_iota(jnp.int32, (128, 128), 1) < HEAD_DIM

    def own_copies(j):
        return (
            pltpu.make_async_copy(q_out.at[y, j], q_all.at[y, j], own_s.at[0, j]),
            pltpu.make_async_copy(kv_out.at[y, j], kv_all.at[y, j, pl.ds(2, 8)], own_s.at[1, j]),
        )

    def edge_copies(h, source, j):
        first, last = kv_out.at[h, j, pl.ds(0, 2)], kv_out.at[h, j, pl.ds(6, 2)]
        return (
            remote(
                first, kv_all.at[source, j, pl.ds(10, 2)],
                edge_s.at[0, h, j], edge_r.at[0, source, j], at(x, h, below, c),
            ),
            remote(
                last, kv_all.at[source, j, pl.ds(0, 2)],
                edge_s.at[1, h, j], edge_r.at[1, source, j], at(x, h, above, c),
            ),
        )

    def process(j):
        even = land[2 * j].astype(F32)
        odd = land[2 * j + 1].astype(F32)
        parts = []
        for f in range(8):
            parts += [even[8 * f : 8 * f + 8], odd[8 * f : 8 * f + 8]]
        rows = jnp.concatenate(parts, axis=0)
        tok2[:, j] = rows.astype(BF16).reshape(8, 16, 512)
        here = emb[pl.ds(pl.multiple_of((j % 4) * 16, 16), 16), :]
        rows = (rows.reshape(8, 16, 512) + here[None]).reshape(128, 512)
        unit = rms(rows, gain_one[...])
        query = dot(unit, wq1[...])
        key = dot(unit, wk1[...]) * key_gain_one[...]
        value = dot(unit, wv1[...])
        for hp in range(2):
            lanes = slice(128 * hp, 128 * hp + 128)
            qp, kp, vp = query[:, lanes], key[:, lanes], value[:, lanes]
            q0 = jnp.where(low, qp, 0.0)
            q1 = jnp.where(low, pltpu.roll(qp, 64, 1), 0.0)
            kv0 = jnp.where(low, kp, pltpu.roll(vp, 64, 1))
            kv1 = jnp.where(low, pltpu.roll(kp, 64, 1), vp)
            q_out[2 * hp, j] = q0.astype(BF16).reshape(8, 16, 128)
            q_out[2 * hp + 1, j] = q1.astype(BF16).reshape(8, 16, 128)
            kv_out[2 * hp, j] = kv0.astype(BF16).reshape(8, 16, 128)
            kv_out[2 * hp + 1, j] = kv1.astype(BF16).reshape(8, 16, 128)
        for d in (2, 1, 3):
            h = (y + d) % 4
            remote(
                kv_out.at[h, j], kv_all.at[y, j, pl.ds(2, 8)], kv_s.at[h, j], kv_r.at[y, j], at(x, h, z, c)
            ).start()
            remote(q_out.at[h, j], q_all.at[y, j], q_s.at[h, j], q_r.at[y, j], at(x, h, z, c)).start()
        for d in (2, 1, 3, 0):
            for copy in edge_copies((y + d) % 4, y, j):
                copy.start()
        for copy in own_copies(j):
            copy.start()

    tok_wait(other)
    process(z // 2)

    def step(i, carry):
        j = pair_at(z, i)
        tok_wait(2 * j)
        tok_wait(2 * j + 1)
        process(j)
        return carry

    lax.fori_loop(1, 8, step, 0)

    def all_here(i, carry):
        j = pair_at(z, i)
        for d in range(1, 4):
            h = (y + d) % 4
            remote(
                kv_out.at[h, j], kv_all.at[h, j, pl.ds(2, 8)], kv_s.at[h, j], kv_r.at[h, j], at(x, h, z, c)
            ).wait()
            remote(q_out.at[h, j], q_all.at[h, j], q_s.at[h, j], q_r.at[h, j], at(x, h, z, c)).wait()
        for h in range(4):
            for copy in edge_copies(h, h, j):
                copy.wait()
        for copy in own_copies(j):
            copy.wait()
        return carry

    lax.fori_loop(0, 8, all_here, 0)

    low256 = lax.broadcasted_iota(jnp.int32, (256, 128), 1) < HEAD_DIM
    low_row = lax.broadcasted_iota(jnp.int32, (1, 128), 1) < HEAD_DIM
    ones_low = jnp.where(low_row, 1.0, 0.0).astype(BF16)
    keep_high = jnp.where(low_row, 0.0, 1.0).astype(BF16)

    def attend(f):
        t = z * 8 + f
        scene_here = scene[t]
        bias = []
        for e in range(5):
            u = t + e - 2
            there = scene[jnp.clip(u, 0, 127)]
            inside = jnp.logical_and(u >= 0, u < 128)
            bias.append(jnp.where(jnp.logical_and(inside, there == scene_here), 0.0, -jnp.inf).astype(F32))
        outs = []
        for sh in range(2):
            pairs = slice(4 * sh, 4 * sh + 4)
            query = q_all[:, pairs, f].reshape(256, 128)
            keys = [kv_all[:, pairs, f + e].reshape(256, 128) for e in range(5)]
            scores = [dot_t(query, keys[e]) for e in range(5)]
            tops = [jnp.max(scores[e], axis=1, keepdims=True) * EXP_SCALE for e in range(5)]
            top = functools.reduce(jnp.maximum, [tops[e] + bias[e] for e in range(5)])
            raised = [jnp.exp2(scores[e] * EXP_SCALE - (top - bias[e])).astype(BF16) for e in range(5)]
            values = [keys[e] * keep_high + ones_low for e in range(5)]
            both = dot(jnp.concatenate(raised, axis=1), jnp.concatenate(values, axis=0))
            turned = pltpu.roll(both, 64, 1)
            outs.append(turned / both if sh == 0 else both / turned)
        whole = jnp.where(low256, outs[0], outs[1])
        mixed[:, f] = whole.astype(BF16).reshape(4, 4, 16, 128)

    def heads_own(k):
        frames = pl.ds(2 * k, 2)
        return pltpu.make_async_copy(mixed.at[y, frames], heads.at[y, frames], turn_s.at[k])

    def send_heads(k):
        frames = pl.ds(2 * k, 2)
        for d in (2, 1, 3):
            t = (y + d) % 4
            remote(
                mixed.at[t, frames], heads.at[y, frames], h_s.at[t, k], h_r.at[y, k], at(x, t, z, c)
            ).start()
        heads_own(k).start()

    low64 = lax.broadcasted_iota(jnp.int32, (64, 128), 1) < HEAD_DIM

    def normed_copy(f):
        return remote(normed.at[f], group.at[me], n_s.at[f], n_r.at[me], at(f // 2, y, z, f % 2))

    def a_copy(t, k):
        return remote(za.at[t, k], back_a.at[z, k], a_s.at[t, k], a_r.at[z, k], at(x, y, t, c))

    def project(k):
        frames = pl.ds(2 * k, 2)
        for d in range(1, 4):
            t = (y + d) % 4
            remote(
                mixed.at[t, frames], heads.at[t, frames], h_s.at[t, k], h_r.at[t, k], at(x, t, z, c)
            ).wait()
        heads_own(k).wait()
        mixes = []
        for parity in range(2):
            part = [heads[h, 2 * k + parity].reshape(64, 128).astype(F32) for h in range(HEADS)]
            for sh in range(2):
                lanes = []
                for hp in range(2):
                    first, second = part[2 * hp], part[2 * hp + 1]
                    if sh == 0:
                        lanes.append(jnp.where(low64, first, pltpu.roll(second, 64, 1)))
                    else:
                        lanes.append(jnp.where(low64, pltpu.roll(first, 64, 1), second))
                mixes.append(jnp.concatenate(lanes, axis=1))
        for sh in range(2):
            for sl in range(8):
                rows = slice(8 * sl, 8 * sl + 8)
                two = jnp.concatenate([mixes[sh][rows], mixes[2 + sh][rows]], axis=0)
                za[8 * sh + sl, k] = two.astype(BF16)
        rows = jnp.concatenate(mixes, axis=0).astype(BF16)
        update = dot(rows, out_one[...])
        residual = tok2[frames].astype(F32).reshape(4, 64, 512) + emb[...][None]
        after = residual.reshape(256, 512) + update
        normed[frames] = rms(after, gain_two[...]).reshape(2, 2, 64, 512)

    def send_a(k):
        a_copy(other, k).start()

        def send(i, carry):
            j = pair_at(z, i)
            a_copy(2 * j, k).start()
            a_copy(2 * j + 1, k).start()
            return carry

        lax.fori_loop(1, 8, send, 0)
        back_a[z, k] = za[z, k]

    def two_frames(i, carry):
        k = (x + 1 + i) % 4

        def one(parity, inner):
            attend(2 * k + parity)
            return inner

        lax.fori_loop(0, 2, one, 0)
        send_heads(k)

        @pl.when(i > 0)
        def _():
            done = (x + i) % 4
            project(done)
            normed_copy(2 * done).start()
            normed_copy(2 * done + 1).start()
            send_a(done)

        return carry

    lax.fori_loop(0, 4, two_frames, 0)
    project(x)
    normed_copy(2 * x + 1 - c).start()
    send_a(x)
    group[me] = normed[me]

    def qkv(s):
        rows = group[s].reshape(128, 512)
        query = dot(rows, wq2[...]).astype(BF16).reshape(2, 4, 16, 256)
        key = (dot(rows, wk2[...]) * key_gain_two[...]).astype(BF16).reshape(2, 4, 16, 256)
        value = dot(rows, wv2[...]).astype(BF16).reshape(2, 4, 16, 256)
        for sh in range(2):
            q2[:, 2 * s + sh] = query[sh]
            k2[:, 2 * s + sh] = key[sh]
            v2[:, 2 * s + sh] = value[sh]

    qkv(me)

    def qkv_step(i, carry):
        s = (me + i) % 8
        remote(normed.at[s], group.at[s], n_s.at[s], n_r.at[s], at(s // 2, y, z, s % 2)).wait()
        qkv(s)
        return carry

    lax.fori_loop(1, 8, qkv_step, 0)
    row = lax.broadcasted_iota(jnp.int32, (256, 256), 0) % 16
    column = lax.broadcasted_iota(jnp.int32, (256, 256), 1)
    alike = row == column % 16
    head_of = column // HEAD_DIM

    def cross(g):
        query = q2[g].reshape(256, 256)
        key = k2[g].reshape(256, 256)
        value = v2[g].reshape(256, 256)
        result = jnp.zeros((256, 256), F32)
        for h in range(HEADS):
            mine = head_of == h
            one = jnp.where(mine, query.astype(F32), 0.0).astype(BF16)
            scores = jnp.where(alike, dot_t(one, key), -jnp.inf)
            top = jnp.max(scores, axis=1, keepdims=True)
            raised = jnp.exp2((scores - top) * EXP_SCALE)
            total = jnp.sum(raised, axis=1, keepdims=True)
            result = jnp.where(mine, dot(raised.astype(BF16), value) / total, result)
        crossed[g] = result.astype(BF16).reshape(8, 2, 16, 256)

    def b_copy(t):
        return remote(zb.at[t], back_b.at[z], b_s.at[t], b_r.at[z], at(x, y, t, c))

    def send_crossed(g):
        def send(i, carry):
            s = (me + i) % 8
            remote(
                crossed.at[g, s], returned.at[g, me], x_s.at[g, s], x_r.at[g, me], at(s // 2, y, z, s % 2)
            ).start()
            return carry

        lax.fori_loop(1, 8, send, 0)
        returned[g, me] = crossed[g, me]

    def send_b(g):
        def wait(i, carry):
            s = (me + i) % 8
            remote(
                crossed.at[g, s], returned.at[g, s], x_s.at[g, s], x_r.at[g, s], at(s // 2, y, z, s % 2)
            ).wait()
            return carry

        lax.fori_loop(1, 8, wait, 0)
        for sh in range(2):
            block = returned[g, :, sh].astype(F32)
            for parity in range(2):
                rows = slice(8 * parity, 8 * parity + 8)
                whole = jnp.concatenate([block[f, rows] for f in range(8)], axis=0)
                t = 8 * sh + 2 * g + parity
                zb[t] = whole.astype(BF16).reshape(4, 16, 256)

                @pl.when(t != z)
                def _(t=t):
                    b_copy(t).start()

    def one_group(i, carry):
        g = (z // 2 + i) % 4
        cross(g)
        send_crossed(g)

        @pl.when(i > 0)
        def _():
            send_b((z // 2 + i + 3) % 4)

        return carry

    lax.fori_loop(0, 4, one_group, 0)
    send_b((z // 2 + 3) % 4)
    back_b[z] = zb[z]

    def tok_done(d, carry):
        tok_copy((z + d) % 16).wait_send()
        return carry

    lax.fori_loop(1, 16, tok_done, 0)

    def finish(d, carry):
        s = (z + d) % 16
        for k in range(4):
            remote(za.at[s, k], back_a.at[s, k], a_s.at[s, k], a_r.at[s, k], at(x, y, s, c)).wait()
        remote(zb.at[s], back_b.at[s], b_s.at[s], b_r.at[s], at(x, y, s, c)).wait()
        return carry

    lax.fori_loop(1, 16, finish, 0)


def final_kernel(tok, ids, table, back_a, back_b, out_one, out_two, out):
    emb = one_hot_rows(ids[...], table[...])

    def step(i, carry):
        four = pl.ds(4 * i, 4)
        rows = tok[four].astype(F32).reshape(32, 8, 512) + emb[None]
        mixed_a = back_a[four].reshape(256, 256)
        mixed_b = back_b[four].reshape(256, 256)
        whole = rows.reshape(256, 512) + dot(mixed_a, out_one[...]) + dot(mixed_b, out_two[...])
        turned = jnp.transpose(whole.reshape(32, 8, 512), (1, 0, 2))
        out[:, pl.ds(pl.multiple_of(i * 32, 32), 32), :] = turned
        return carry

    lax.fori_loop(0, 4, step, 0)


VMEM = pl.BlockSpec(memory_space=pltpu.VMEM)
SMEM = pl.BlockSpec(memory_space=pltpu.SMEM)
DMA = pltpu.SemaphoreType.DMA


def shape(*dims, dtype=BF16):
    return jax.ShapeDtypeStruct(dims, dtype)


def params(**more):
    return pltpu.CompilerParams(vmem_limit_bytes=40 << 20, **more)


def on_device(
    tokens, patch_ids, patch_embed, scene_ids,
    norm_one, query_one, key_one, value_one, key_gain_one, out_one,
    norm_two, query_two, key_two, value_two, key_gain_two, out_two,
):
    tok = jnp.transpose(tokens.reshape(8, 16, 8, 512), (1, 2, 0, 3)).reshape(16, 64, 512)
    ids = jnp.broadcast_to(patch_ids[:, None], (8, 128))
    back_a, back_b = pl.pallas_call(
        layer_kernel,
        out_shape=(shape(16, 4, 16, 256), shape(16, 4, 16, 256)),
        in_specs=[SMEM] + [VMEM] * 14,
        out_specs=(VMEM,) * 2,
        scratch_shapes=[
            pltpu.VMEM((16, 64, 512), BF16),
            pltpu.VMEM((8, 8, 128), jnp.int32),
            pltpu.VMEM((64, 512), F32),
            pltpu.VMEM((8, 8, 16, 512), BF16),
            pltpu.VMEM((4, 8, 8, 16, 128), BF16),
            pltpu.VMEM((4, 8, 8, 16, 128), BF16),
            pltpu.VMEM((4, 8, 8, 16, 128), BF16),
            pltpu.VMEM((4, 8, 12, 16, 128), BF16),
            pltpu.VMEM((4, 8, 4, 16, 128), BF16),
            pltpu.VMEM((4, 8, 4, 16, 128), BF16),
            pltpu.VMEM((16, 4, 16, 256), BF16),
            pltpu.VMEM((16, 4, 16, 256), BF16),
            pltpu.VMEM((8, 2, 64, 512), BF16),
            pltpu.VMEM((8, 2, 64, 512), BF16),
            pltpu.VMEM((4, 16, 16, 256), BF16),
            pltpu.VMEM((4, 16, 16, 256), BF16),
            pltpu.VMEM((4, 16, 16, 256), BF16),
            pltpu.VMEM((4, 8, 2, 16, 256), BF16),
            pltpu.VMEM((4, 8, 2, 16, 256), BF16),
            DMA((16,)), DMA((16,)), DMA((8,)), DMA((8,)),
            DMA((4, 8)), DMA((4, 8)), DMA((4, 8)), DMA((4, 8)), DMA((2, 8)), DMA((2, 4, 8)), DMA((2, 4, 8)),
            DMA((4, 4)), DMA((4, 4)), DMA((8,)), DMA((8,)), DMA((4, 8)), DMA((4, 8)),
            DMA((16, 4)), DMA((16, 4)), DMA((16,)), DMA((16,)), DMA((4,)),
        ],
        compiler_params=params(collective_id=0, has_side_effects=True),
        name="layer",
    )(
        scene_ids, tok, ids, patch_embed, norm_one[None], query_one, key_one, value_one, key_gain_one[None],
        out_one, norm_two[None], query_two, key_two, value_two, key_gain_two[None],
    )
    out = pl.pallas_call(
        final_kernel,
        out_shape=shape(8, 128, 512, dtype=F32),
        in_specs=[VMEM] * 7,
        out_specs=VMEM,
        compiler_params=params(),
        name="final",
    )(tok, ids, patch_embed, back_a, back_b, out_one, out_two)
    return out.reshape(1, 8, 128, 512)


def solution(mesh):
    return jax.shard_map(
        on_device,
        mesh=mesh,
        in_specs=(P("subj", "patch", None, None), P("patch")) + (P(),) * 14,
        out_specs=P("subj", "patch", None, None),
        check_vma=False,
    )
```

```python
import functools
import math

import jax
import jax.numpy as jnp
from jax import lax
from jax.experimental import pallas as pl
from jax.experimental.pallas import tpu as pltpu
from jax.sharding import PartitionSpec as P

MESH = pl.DeviceIdType.MESH
HEADS = 4
HEAD_DIM = 64
EPS = 1e-05
F32 = jnp.float32
BF16 = jnp.bfloat16
EXP_SCALE = math.log2(math.e) / math.sqrt(HEAD_DIM)


def coords():
    s = lax.axis_index("subj")
    p = lax.axis_index("patch")
    return s // 4, p // 8, ((s // 2) % 2) * 8 + p % 8, s % 2


def at(x, y, z, c):
    return ((x * 2 + z // 8) * 2 + c, y * 8 + z % 8)


def remote(src, dst, send, recv, device):
    return pltpu.make_async_remote_copy(
        src_ref=src, dst_ref=dst, send_sem=send, recv_sem=recv, device_id=device, device_id_type=MESH
    )


def pair_at(z, i):
    half = (i + 1) // 2
    sign = 2 * (i % 2) - 1
    return (z // 2 + 8 + sign * half) % 8


def sent(ref, sem, device):
    remote(ref, ref, sem, sem, device).wait_send()


def arrived(ref, sem, device):
    remote(ref, ref, sem, sem, device).wait_recv()


def rms(rows, gain):
    mean = jnp.mean(rows * rows, axis=-1, keepdims=True)
    return (rows * lax.rsqrt(mean + EPS) * gain).astype(BF16)


def dot(a, b):
    return jnp.dot(a, b, preferred_element_type=F32)


def dot_t(a, b):
    return lax.dot_general(a, b, (((1,), (1,)), ((), ())), preferred_element_type=F32)


def id_rows(ids):
    row = lax.broadcasted_iota(jnp.int32, (8, 128), 0)
    spread = jnp.zeros((8, 128), jnp.int32)
    for p in range(8):
        spread = jnp.where(row == p, ids[p], spread)
    return spread


def one_hot_rows(ids, table):
    lane = lax.broadcasted_iota(jnp.int32, ids.shape, 1)
    low = jnp.where(ids == lane, 1.0, 0.0).astype(F32)
    high = jnp.where(ids == lane + 128, 1.0, 0.0).astype(F32)
    picked = jnp.concatenate([low, high], axis=1).astype(BF16)
    return dot(picked, table)


def layer_kernel(
    scene, ids, tok, table, gain_one, wq1, wk1, wv1, key_gain_one, out_one, gain_two, wq2, wk2, wv2, key_gain_two,
    back_a, back_b,
    land, ids_land, emb, tok2, q_out, kv_out, q_all, kv_all, mixed, heads, za, zb, normed, group, q2, k2, v2,
    crossed, returned,
    tok_s, tok_r, ids_s, ids_r, q_s, q_r, kv_s, kv_r, own_s, edge_s, edge_r, h_s, h_r, n_s, n_r, x_s, x_r,
    a_s, a_r, b_s, b_r, turn_s, own_tok_s,
):
    x, y, z, c = coords()
    zh, zl = z // 8, z % 8
    me = x * 2 + c
    other = z + 1 - 2 * (z % 2)
    buddy = at(x, y, other, c)
    three, seven, fifteen = pl.ds(0, 3), pl.ds(0, 7), pl.ds(0, 15)
    below, above = (z + 15) % 16, (z + 1) % 16
    barrier = pltpu.get_barrier_semaphore()

    def greet(device):
        pl.semaphore_signal(barrier, inc=1, device_id=device, device_id_type=MESH)

    for d in range(1, 16):
        greet(at(x, y, (z + d) % 16, c))
    for d in range(1, 4):
        for near in (z, below, above):
            greet(at(x, (y + d) % 4, near, c))
    for d in range(1, 8):
        t = (me + d) % 8
        greet(at(t // 2, y, z, t % 2))
    pl.semaphore_wait(barrier, 31)

    def tok_copy(t):
        return remote(tok.at[:, t], land.at[z], tok_s, tok_r.at[z // 2], at(x, y, t, c))

    def pair_wait(j):
        arrived(land.at[pl.ds(2 * j, 2)], tok_r.at[j], buddy)

    tok_copy(other).start()
    ids_land[zl] = id_rows(ids)
    for d in range(1, 8):
        t = zh * 8 + (zl + d) % 8
        remote(ids_land.at[zl], ids_land.at[zl], ids_s, ids_r, at(x, y, t, c)).start()

    def send_pair(i, carry):
        j = pair_at(z, i)
        tok_copy(2 * j).start()
        tok_copy(2 * j + 1).start()
        return carry

    lax.fori_loop(1, 8, send_pair, 0)
    own_tok = pltpu.make_async_copy(tok.at[:, z], land.at[z], own_tok_s)
    own_tok.start()
    sent(ids_land.at[seven], ids_s, buddy)
    arrived(ids_land.at[seven], ids_r, buddy)
    emb[...] = one_hot_rows(ids_land[...].reshape(64, 128), table[...])
    own_tok.wait()

    low = lax.broadcasted_iota(jnp.int32, (128, 128), 1) < HEAD_DIM
    low64 = lax.broadcasted_iota(jnp.int32, (64, 128), 1) < HEAD_DIM

    def own_copies(j):
        return (
            pltpu.make_async_copy(q_out.at[y, j], q_all.at[y, j], own_s.at[0, j // 4]),
            pltpu.make_async_copy(kv_out.at[y, j], kv_all.at[y, j, pl.ds(2, 8)], own_s.at[1, j // 4]),
        )

    def send_edges(sh):
        pairs = pl.ds(4 * sh, 4)
        for d in (2, 1, 3, 0):
            h = (y + d) % 4
            remote(
                kv_out.at[h, pairs, pl.ds(0, 2)], kv_all.at[y, pairs, pl.ds(10, 2)],
                edge_s, edge_r.at[0, sh], at(x, h, below, c),
            ).start()
            remote(
                kv_out.at[h, pairs, pl.ds(6, 2)], kv_all.at[y, pairs, pl.ds(0, 2)],
                edge_s, edge_r.at[1, sh], at(x, h, above, c),
            ).start()

    def edge_here(side, sh):
        arrived(kv_all.at[:, pl.ds(4 * sh, 4), pl.ds(10 - 10 * side, 2)], edge_r.at[side, sh], buddy)

    def process(j):
        rows = jnp.transpose(land[pl.ds(2 * j, 2)].astype(F32).reshape(16, 8, 512), (1, 0, 2))
        tok2[:, j] = rows.astype(BF16)
        here = emb[pl.ds(pl.multiple_of((j % 4) * 16, 16), 16), :]
        rows = (rows + here[None]).reshape(128, 512)
        unit = rms(rows, gain_one[...])
        query = dot(unit, wq1[...])
        key = dot(unit, wk1[...]) * key_gain_one[...]
        value = dot(unit, wv1[...])
        for hp in range(2):
            lanes = slice(128 * hp, 128 * hp + 128)
            qp, kp, vp = query[:, lanes], key[:, lanes], value[:, lanes]
            qp = qp.reshape(4, 2, 16, 128)
            first, second = qp[:, 0].reshape(64, 128), qp[:, 1].reshape(64, 128)
            q0 = jnp.where(low64, first, pltpu.roll(second, 64, 1))
            q1 = jnp.where(low64, pltpu.roll(first, 64, 1), second)
            kv0 = jnp.where(low, kp, pltpu.roll(vp, 64, 1))
            kv1 = jnp.where(low, pltpu.roll(kp, 64, 1), vp)
            q_out[2 * hp, j] = q0.astype(BF16).reshape(4, 16, 128)
            q_out[2 * hp + 1, j] = q1.astype(BF16).reshape(4, 16, 128)
            kv_out[2 * hp, j] = kv0.astype(BF16).reshape(8, 16, 128)
            kv_out[2 * hp + 1, j] = kv1.astype(BF16).reshape(8, 16, 128)
        for d in (2, 1, 3):
            h = (y + d) % 4
            remote(
                kv_out.at[h, j], kv_all.at[y, j, pl.ds(2, 8)], kv_s, kv_r.at[j // 4], at(x, h, z, c)
            ).start()
            remote(q_out.at[h, j], q_all.at[y, j], q_s, q_r.at[j // 4], at(x, h, z, c)).start()
        for copy in own_copies(j):
            copy.start()

    arrived(land.at[other], tok_r.at[z // 2], buddy)
    process(z // 2)

    first_pairs = 6 - 2 * ((zl // 2 + 3) // 4) + zl // 4 + 2 * (zl // 6)

    def first_step(i, carry):
        j = pair_at(z, i)
        pair_wait(j)
        process(j)
        return carry

    lax.fori_loop(1, first_pairs, first_step, 0)

    send_edges(zh)
    lax.fori_loop(first_pairs, 8, first_step, 0)
    send_edges(1 - zh)

    def all_here(sh):
        pairs = pl.ds(4 * sh, 4)
        arrived(kv_all.at[three, pairs, pl.ds(2, 8)], kv_r.at[sh], buddy)
        arrived(q_all.at[three, pairs], q_r.at[sh], buddy)
        pltpu.make_async_copy(q_out.at[y, pairs], q_all.at[y, pairs], own_s.at[0, sh]).wait()
        pltpu.make_async_copy(
            kv_out.at[y, pairs], kv_all.at[y, pairs, pl.ds(2, 8)], own_s.at[1, sh]
        ).wait()

    low256 = lax.broadcasted_iota(jnp.int32, (256, 128), 1) < HEAD_DIM
    low_row = lax.broadcasted_iota(jnp.int32, (1, 128), 1) < HEAD_DIM
    ones_low = jnp.where(low_row, 1.0, 0.0).astype(BF16)
    keep_high = jnp.where(low_row, 0.0, 1.0).astype(BF16)

    def attend(sh, k):
        pairs = pl.ds(4 * sh, 4)
        packed = q_all[:, pairs, k].reshape(256, 128).astype(F32)
        keys = [kv_all[:, pairs, 2 * k + e].reshape(256, 128) for e in range(6)]
        values = [one * keep_high + ones_low for one in keys]
        outs = []
        for parity in range(2):
            t = z * 8 + 2 * k + parity
            scene_here = scene[t]
            bias = []
            for e in range(5):
                u = t + e - 2
                there = scene[jnp.clip(u, 0, 127)]
                inside = jnp.logical_and(u >= 0, u < 128)
                bias.append(jnp.where(jnp.logical_and(inside, there == scene_here), 0.0, -jnp.inf).astype(F32))
            turned = packed if parity == 0 else pltpu.roll(packed, 64, 1)
            query = jnp.where(low256, turned, 0.0).astype(BF16)
            scores = [dot_t(query, keys[parity + e]) for e in range(5)]
            tops = [jnp.maximum(one[:, :128], one[:, 128:]) + bias[e] for e, one in enumerate(scores)]
            top = jnp.max(functools.reduce(jnp.maximum, tops), axis=1, keepdims=True) * EXP_SCALE
            raised = [
                jnp.exp2(one * EXP_SCALE - (top - bias[e])).astype(BF16) for e, one in enumerate(scores)
            ]
            both = dot(jnp.concatenate(raised, axis=1), jnp.concatenate(values[parity : parity + 5], axis=0))
            other_way = pltpu.roll(both, 64, 1)
            outs.append(other_way / both if parity == 0 else both / other_way)
        whole = jnp.where(low256, outs[0], outs[1])
        mixed[sh, :, k] = whole.astype(BF16).reshape(4, 4, 16, 128)

    def heads_own(sh, k):
        return pltpu.make_async_copy(mixed.at[sh, y, k], heads.at[sh, y, k], turn_s.at[sh, k])

    def send_heads(sh, k):
        for d in (2, 1, 3):
            t = (y + d) % 4
            remote(
                mixed.at[sh, t, k], heads.at[sh, y, k], h_s, h_r.at[sh, k], at(x, t, z, c)
            ).start()
        heads_own(sh, k).start()

    def normed_copy(sh, f):
        return remote(
            normed.at[f, sh], group.at[me, sh], n_s, n_r.at[sh, x], at(f // 2, y, z, f % 2)
        )

    def a_part(t, k):
        return remote(za.at[t, k], back_a.at[z, k], a_s, a_r, at(x, y, t, c))

    def project(sh, k):
        arrived(heads.at[sh, three, k], h_r.at[sh, k], buddy)
        heads_own(sh, k).wait()
        part = [heads[sh, h, k].reshape(64, 128).astype(F32) for h in range(HEADS)]
        mixes = []
        for parity in range(2):
            lanes = []
            for hp in range(2):
                first, second = part[2 * hp], part[2 * hp + 1]
                if parity == 0:
                    lanes.append(jnp.where(low64, first, pltpu.roll(second, 64, 1)))
                else:
                    lanes.append(jnp.where(low64, pltpu.roll(first, 64, 1), second))
            mixes.append(jnp.concatenate(lanes, axis=1))
        for sl in range(8):
            rows = slice(8 * sl, 8 * sl + 8)
            two = jnp.concatenate([mixes[0][rows], mixes[1][rows]], axis=0)
            za[8 * sh + sl, k] = two.astype(BF16)
        rows = jnp.concatenate(mixes, axis=0).astype(BF16)
        update = dot(rows, out_one[...])
        held = tok2[pl.ds(2 * k, 2), pl.ds(4 * sh, 4)].astype(F32)
        after = (held.reshape(2, 64, 512) + emb[...][None]).reshape(128, 512) + update
        normed[pl.ds(2 * k, 2), sh] = rms(after, gain_two[...]).reshape(2, 64, 512)

    def send_normed(sh, k):
        normed_copy(sh, 2 * k).start()
        normed_copy(sh, 2 * k + 1).start()

    def send_last(sh):
        normed_copy(sh, 2 * x + 1 - c).start()
        group[me, sh] = normed[me, sh]

    def send_a(k):
        a_part(other, k).start()

        def send(i, carry):
            j = pair_at(z, i)
            a_part(2 * j, k).start()
            a_part(2 * j + 1, k).start()
            return carry

        lax.fori_loop(1, 8, send, 0)
        back_a[z, k] = za[z, k]

    for sh in range(2):
        all_here(sh)
        edge_here(0, sh)
        edge_here(1, sh)

    def two_frames(i, carry):
        k = (x + 1 + i) % 4

        def one(sh, inner):
            attend(sh, k)
            send_heads(sh, k)
            return inner

        lax.fori_loop(0, 2, one, 0)

        @pl.when(i > 0)
        def _():
            done = (x + i) % 4
            for sh in range(2):
                project(sh, done)
                send_normed(sh, done)
            send_a(done)

        return carry

    lax.fori_loop(0, 4, two_frames, 0)
    for sh in range(2):
        project(sh, x)
        send_last(sh)
    send_a(x)

    def qkv(xs, sh):
        rows = group[pl.ds(2 * xs, 2), sh].reshape(128, 512)
        query = dot(rows, wq2[...]).astype(BF16).reshape(2, 4, 16, 256)
        key = (dot(rows, wk2[...]) * key_gain_two[...]).astype(BF16).reshape(2, 4, 16, 256)
        value = dot(rows, wv2[...]).astype(BF16).reshape(2, 4, 16, 256)
        for core in range(2):
            q2[:, 4 * xs + 2 * core + sh] = query[core]
            k2[:, 4 * xs + 2 * core + sh] = key[core]
            v2[:, 4 * xs + 2 * core + sh] = value[core]

    def all_qkv(sh):
        arrived(group.at[2 * x + 1 - c, sh], n_r.at[sh, x], buddy)
        qkv(x, sh)

        def next_x(i, carry):
            xs = (x + i) % 4
            arrived(group.at[pl.ds(2 * xs, 2), sh], n_r.at[sh, xs], buddy)
            qkv(xs, sh)
            return carry

        lax.fori_loop(1, 4, next_x, 0)

    all_qkv(0)
    all_qkv(1)

    row = lax.broadcasted_iota(jnp.int32, (256, 256), 0) % 16
    column = lax.broadcasted_iota(jnp.int32, (256, 256), 1)
    alike = row == column % 16
    head_of = column // HEAD_DIM

    def cross(g):
        query = q2[g].reshape(256, 256)
        key = k2[g].reshape(256, 256)
        value = v2[g].reshape(256, 256)
        result = jnp.zeros((256, 256), F32)
        for h in range(HEADS):
            mine = head_of == h
            one = jnp.where(mine, query.astype(F32), 0.0).astype(BF16)
            scores = jnp.where(alike, dot_t(one, key), -jnp.inf)
            top = jnp.max(scores, axis=1, keepdims=True)
            raised = jnp.exp2((scores - top) * EXP_SCALE)
            total = jnp.sum(raised, axis=1, keepdims=True)
            result = jnp.where(mine, dot(raised.astype(BF16), value) / total, result)
        crossed[g] = result.astype(BF16).reshape(8, 2, 16, 256)

    def b_copy(t):
        return remote(zb.at[t], back_b.at[z], b_s, b_r, at(x, y, t, c))

    def send_crossed(g):
        def send(i, carry):
            s = (me + i) % 8
            remote(
                crossed.at[g, s], returned.at[g, me], x_s, x_r.at[g], at(s // 2, y, z, s % 2)
            ).start()
            return carry

        lax.fori_loop(1, 8, send, 0)
        returned[g, me] = crossed[g, me]

    def send_b(g):
        arrived(returned.at[g, seven], x_r.at[g], buddy)
        for sh in range(2):
            block = returned[g, :, sh].astype(F32)
            for parity in range(2):
                rows = slice(8 * parity, 8 * parity + 8)
                whole = jnp.concatenate([block[f, rows] for f in range(8)], axis=0)
                t = 8 * sh + 2 * g + parity
                zb[t] = whole.astype(BF16).reshape(4, 16, 256)

                @pl.when(t != z)
                def _(t=t):
                    b_copy(t).start()

    def one_group(i, carry):
        g = (z // 2 + i) % 4
        cross(g)
        send_crossed(g)

        @pl.when(i > 0)
        def _():
            send_b((z // 2 + i + 3) % 4)

        return carry

    lax.fori_loop(0, 4, one_group, 0)
    send_b((z // 2 + 3) % 4)
    back_b[z] = zb[z]

    sent(land.at[fifteen], tok_s, buddy)
    sent(kv_out.at[three], kv_s, buddy)
    sent(q_out.at[three], q_s, buddy)
    sent(kv_out.at[:, :, pl.ds(0, 4)], edge_s, buddy)
    sent(mixed.at[:, three], h_s, buddy)
    sent(normed.at[seven], n_s, buddy)
    sent(crossed.at[:, seven], x_s, buddy)
    sent(za.at[fifteen], a_s, buddy)
    sent(zb.at[fifteen], b_s, buddy)
    arrived(back_a.at[fifteen], a_r, buddy)
    arrived(back_b.at[fifteen], b_r, buddy)


def final_kernel(ids, tok, table, back_a, back_b, out_one, out_two, out, emb):
    @pl.when(pl.program_id(0) == 0)
    def _():
        emb[...] = one_hot_rows(id_rows(ids), table[...])

    mixed_a = back_a[...].reshape(512, 256)
    mixed_b = back_b[...].reshape(512, 256)
    update = dot(mixed_a, out_one[...]) + dot(mixed_b, out_two[...])
    rows = tok[...].astype(F32) + emb[...][:, None]
    out[...] = rows + jnp.transpose(update.reshape(64, 8, 512), (1, 0, 2))


VMEM = pl.BlockSpec(memory_space=pltpu.VMEM)
SMEM = pl.BlockSpec(memory_space=pltpu.SMEM)
DMA = pltpu.SemaphoreType.DMA


def shape(*dims, dtype=BF16):
    return jax.ShapeDtypeStruct(dims, dtype)


def params(**more):
    return pltpu.CompilerParams(vmem_limit_bytes=60 << 20, **more)


def on_device(
    tokens, patch_ids, patch_embed, scene_ids,
    norm_one, query_one, key_one, value_one, key_gain_one, out_one,
    norm_two, query_two, key_two, value_two, key_gain_two, out_two,
):
    tok = tokens.reshape(8, 16, 8, 512)
    back_a, back_b = pl.pallas_call(
        layer_kernel,
        out_shape=(shape(16, 4, 16, 256), shape(16, 4, 16, 256)),
        in_specs=[SMEM, SMEM, pl.BlockSpec(memory_space=pl.ANY)] + [VMEM] * 12,
        out_specs=(VMEM,) * 2,
        scratch_shapes=[
            pltpu.VMEM((16, 8, 8, 512), BF16),
            pltpu.VMEM((8, 8, 128), jnp.int32),
            pltpu.VMEM((64, 512), F32),
            pltpu.VMEM((8, 8, 16, 512), BF16),
            pltpu.VMEM((4, 8, 4, 16, 128), BF16),
            pltpu.VMEM((4, 8, 8, 16, 128), BF16),
            pltpu.VMEM((4, 8, 4, 16, 128), BF16),
            pltpu.VMEM((4, 8, 12, 16, 128), BF16),
            pltpu.VMEM((2, 4, 4, 4, 16, 128), BF16),
            pltpu.VMEM((2, 4, 4, 4, 16, 128), BF16),
            pltpu.VMEM((16, 4, 16, 256), BF16),
            pltpu.VMEM((16, 4, 16, 256), BF16),
            pltpu.VMEM((8, 2, 64, 512), BF16),
            pltpu.VMEM((8, 2, 64, 512), BF16),
            pltpu.VMEM((4, 16, 16, 256), BF16),
            pltpu.VMEM((4, 16, 16, 256), BF16),
            pltpu.VMEM((4, 16, 16, 256), BF16),
            pltpu.VMEM((4, 8, 2, 16, 256), BF16),
            pltpu.VMEM((4, 8, 2, 16, 256), BF16),
            DMA, DMA((8,)), DMA, DMA, DMA, DMA((2,)), DMA, DMA((2,)), DMA((2, 2)), DMA, DMA((2, 2)),
            DMA, DMA((2, 4)), DMA, DMA((2, 4)), DMA, DMA((4,)),
            DMA, DMA, DMA, DMA, DMA((2, 4)), DMA,
        ],
        compiler_params=params(collective_id=0, has_side_effects=True),
        name="layer",
    )(
        scene_ids, patch_ids, tok, patch_embed, norm_one[None], query_one, key_one, value_one, key_gain_one[None],
        out_one, norm_two[None], query_two, key_two, value_two, key_gain_two[None],
    )
    out = pl.pallas_call(
        final_kernel,
        grid=(2,),
        out_shape=shape(8, 128, 512, dtype=F32),
        in_specs=[
            SMEM,
            pl.BlockSpec((8, 64, 512), lambda i: (0, i, 0)),
            VMEM,
            pl.BlockSpec((8, 4, 16, 256), lambda i: (i, 0, 0, 0)),
            pl.BlockSpec((8, 4, 16, 256), lambda i: (i, 0, 0, 0)),
            VMEM,
            VMEM,
        ],
        out_specs=pl.BlockSpec((8, 64, 512), lambda i: (0, i, 0)),
        scratch_shapes=[pltpu.VMEM((8, 512), F32)],
        compiler_params=params(),
        name="final",
    )(patch_ids, tokens[0], patch_embed, back_a, back_b, out_one, out_two)
    return out.reshape(1, 8, 128, 512)


def solution(mesh):
    return jax.shard_map(
        on_device,
        mesh=mesh,
        in_specs=(P("subj", "patch", None, None), P("patch")) + (P(),) * 14,
        out_specs=P("subj", "patch", None, None),
        check_vma=False,
    )
```

```python
import functools
import math

import jax
import jax.numpy as jnp
from jax import lax
from jax.experimental import pallas as pl
from jax.experimental.pallas import tpu as pltpu
from jax.sharding import PartitionSpec as P

MESH = pl.DeviceIdType.MESH
HEADS = 4
HEAD_DIM = 64
EPS = 1e-05
F32 = jnp.float32
BF16 = jnp.bfloat16
EXP_SCALE = math.log2(math.e) / math.sqrt(HEAD_DIM)


def coords():
    s = lax.axis_index("subj")
    p = lax.axis_index("patch")
    return s // 4, p // 8, ((s // 2) % 2) * 8 + p % 8, s % 2


def at(x, y, z, c):
    return ((x * 2 + z // 8) * 2 + c, y * 8 + z % 8)


def remote(src, dst, send, recv, device):
    return pltpu.make_async_remote_copy(
        src_ref=src, dst_ref=dst, send_sem=send, recv_sem=recv, device_id=device, device_id_type=MESH
    )


def pair_at(z, i):
    half = (i + 1) // 2
    sign = 2 * (i % 2) - 1
    return (z // 2 + 8 + sign * half) % 8


def sent(ref, sem, device):
    remote(ref, ref, sem, sem, device).wait_send()


def arrived(ref, sem, device):
    remote(ref, ref, sem, sem, device).wait_recv()


def rms(rows, gain):
    mean = jnp.mean(rows * rows, axis=-1, keepdims=True)
    return (rows * lax.rsqrt(mean + EPS) * gain).astype(BF16)


def dot(a, b):
    return jnp.dot(a, b, preferred_element_type=F32)


def dot_t(a, b):
    return lax.dot_general(a, b, (((1,), (1,)), ((), ())), preferred_element_type=F32)


def id_rows(ids):
    row = lax.broadcasted_iota(jnp.int32, (8, 128), 0)
    spread = jnp.zeros((8, 128), jnp.int32)
    for p in range(8):
        spread = jnp.where(row == p, ids[p], spread)
    return spread


def one_hot_rows(ids, table):
    lane = lax.broadcasted_iota(jnp.int32, ids.shape, 1)
    low = jnp.where(ids == lane, 1.0, 0.0).astype(F32)
    high = jnp.where(ids == lane + 128, 1.0, 0.0).astype(F32)
    picked = jnp.concatenate([low, high], axis=1).astype(BF16)
    return dot(picked, table)


def layer_kernel(
    scene, ids, tok, table, gain_one, wq1, wk1, wv1, key_gain_one, out_one, gain_two, wq2, wk2, wv2, key_gain_two,
    back_a, back_b,
    land, ids_land, emb, tok2, q_out, kv_out, q_all, kv_all, mixed, heads, za, zb, normed, group, q2, k2, v2,
    crossed, returned,
    tok_s, tok_r, ids_s, ids_r, q_s, q_r, kv_s, kv_r, own_s, edge_s, edge_r, h_s, h_r, n_s, n_r, x_s, x_r,
    a_s, a_r, b_s, b_r, turn_s, own_tok_s,
):
    x, y, z, c = coords()
    zh, zl = z // 8, z % 8
    me = x * 2 + c
    other = z + 1 - 2 * (z % 2)
    buddy = at(x, y, other, c)
    three, seven, fifteen = pl.ds(0, 3), pl.ds(0, 7), pl.ds(0, 15)
    below, above = (z + 15) % 16, (z + 1) % 16
    barrier = pltpu.get_barrier_semaphore()

    def greet(device):
        pl.semaphore_signal(barrier, inc=1, device_id=device, device_id_type=MESH)

    for d in range(1, 16):
        greet(at(x, y, (z + d) % 16, c))
    for d in range(1, 4):
        for near in (z, below, above):
            greet(at(x, (y + d) % 4, near, c))
    for d in range(1, 8):
        t = (me + d) % 8
        greet(at(t // 2, y, z, t % 2))
    pl.semaphore_wait(barrier, 31)

    def tok_copy(t):
        return remote(tok.at[:, t], land.at[z], tok_s, tok_r.at[z // 2], at(x, y, t, c))

    def pair_wait(j):
        arrived(land.at[pl.ds(2 * j, 2)], tok_r.at[j], buddy)

    tok_copy(other).start()
    ids_land[zl] = id_rows(ids)
    for d in range(1, 8):
        t = zh * 8 + (zl + d) % 8
        remote(ids_land.at[zl], ids_land.at[zl], ids_s, ids_r, at(x, y, t, c)).start()

    def send_pair(i, carry):
        j = pair_at(z, i)
        tok_copy(2 * j).start()
        tok_copy(2 * j + 1).start()
        return carry

    lax.fori_loop(1, 8, send_pair, 0)
    own_tok = pltpu.make_async_copy(tok.at[:, z], land.at[z], own_tok_s)
    own_tok.start()
    sent(ids_land.at[seven], ids_s, buddy)
    arrived(ids_land.at[seven], ids_r, buddy)
    emb[...] = one_hot_rows(ids_land[...].reshape(64, 128), table[...])
    own_tok.wait()

    low = lax.broadcasted_iota(jnp.int32, (128, 128), 1) < HEAD_DIM
    low64 = lax.broadcasted_iota(jnp.int32, (64, 128), 1) < HEAD_DIM

    def own_copies(j):
        return (
            pltpu.make_async_copy(q_out.at[y, j], q_all.at[y, j], own_s.at[0, j // 4]),
            pltpu.make_async_copy(kv_out.at[y, j], kv_all.at[y, j, pl.ds(2, 8)], own_s.at[1, j // 4]),
        )

    def send_edges(sh):
        pairs = pl.ds(4 * sh, 4)
        for d in (2, 1, 3, 0):
            h = (y + d) % 4
            remote(
                kv_out.at[h, pairs, pl.ds(0, 2)], kv_all.at[y, pairs, pl.ds(10, 2)],
                edge_s, edge_r.at[0, sh], at(x, h, below, c),
            ).start()
            remote(
                kv_out.at[h, pairs, pl.ds(6, 2)], kv_all.at[y, pairs, pl.ds(0, 2)],
                edge_s, edge_r.at[1, sh], at(x, h, above, c),
            ).start()

    def edge_here(side, sh):
        arrived(kv_all.at[:, pl.ds(4 * sh, 4), pl.ds(10 - 10 * side, 2)], edge_r.at[side, sh], buddy)

    def process(j):
        rows = jnp.transpose(land[pl.ds(2 * j, 2)].astype(F32).reshape(16, 8, 512), (1, 0, 2))
        tok2[:, j] = rows.astype(BF16)
        here = emb[pl.ds(pl.multiple_of((j % 4) * 16, 16), 16), :]
        rows = (rows + here[None]).reshape(128, 512)
        unit = rms(rows, gain_one[...])
        query = dot(unit, wq1[...])
        key = dot(unit, wk1[...]) * key_gain_one[...]
        value = dot(unit, wv1[...])
        for hp in range(2):
            lanes = slice(128 * hp, 128 * hp + 128)
            qp, kp, vp = query[:, lanes], key[:, lanes], value[:, lanes]
            qp = qp.reshape(4, 2, 16, 128)
            first, second = qp[:, 0].reshape(64, 128), qp[:, 1].reshape(64, 128)
            q0 = jnp.where(low64, first, pltpu.roll(second, 64, 1))
            q1 = jnp.where(low64, pltpu.roll(first, 64, 1), second)
            kv0 = jnp.where(low, kp, pltpu.roll(vp, 64, 1))
            kv1 = jnp.where(low, pltpu.roll(kp, 64, 1), vp)
            q_out[2 * hp, j] = q0.astype(BF16).reshape(4, 16, 128)
            q_out[2 * hp + 1, j] = q1.astype(BF16).reshape(4, 16, 128)
            kv_out[2 * hp, j] = kv0.astype(BF16).reshape(8, 16, 128)
            kv_out[2 * hp + 1, j] = kv1.astype(BF16).reshape(8, 16, 128)
        for d in (2, 1, 3):
            h = (y + d) % 4
            remote(
                kv_out.at[h, j], kv_all.at[y, j, pl.ds(2, 8)], kv_s, kv_r.at[j // 4], at(x, h, z, c)
            ).start()
            remote(q_out.at[h, j], q_all.at[y, j], q_s, q_r.at[j // 4], at(x, h, z, c)).start()
        for copy in own_copies(j):
            copy.start()

    arrived(land.at[other], tok_r.at[z // 2], buddy)
    process(z // 2)

    first_pairs = 6 - 2 * ((zl // 2 + 3) // 4) + zl // 4 + 2 * (zl // 6)

    def first_step(i, carry):
        j = pair_at(z, i)
        pair_wait(j)
        process(j)
        return carry

    lax.fori_loop(1, first_pairs, first_step, 0)

    send_edges(zh)
    lax.fori_loop(first_pairs, 8, first_step, 0)
    send_edges(1 - zh)

    def all_here(sh):
        pairs = pl.ds(4 * sh, 4)
        arrived(kv_all.at[three, pairs, pl.ds(2, 8)], kv_r.at[sh], buddy)
        arrived(q_all.at[three, pairs], q_r.at[sh], buddy)
        pltpu.make_async_copy(q_out.at[y, pairs], q_all.at[y, pairs], own_s.at[0, sh]).wait()
        pltpu.make_async_copy(
            kv_out.at[y, pairs], kv_all.at[y, pairs, pl.ds(2, 8)], own_s.at[1, sh]
        ).wait()

    low256 = lax.broadcasted_iota(jnp.int32, (256, 128), 1) < HEAD_DIM
    low_row = lax.broadcasted_iota(jnp.int32, (1, 128), 1) < HEAD_DIM
    ones_low = jnp.where(low_row, 1.0, 0.0).astype(BF16)
    keep_high = jnp.where(low_row, 0.0, 1.0).astype(BF16)

    def attend(sh, k):
        pairs = pl.ds(4 * sh, 4)
        packed = q_all[:, pairs, k].reshape(256, 128).astype(F32)
        keys = [kv_all[:, pairs, 2 * k + e].reshape(256, 128) for e in range(6)]
        values = [one * keep_high + ones_low for one in keys]
        outs = []
        for parity in range(2):
            t = z * 8 + 2 * k + parity
            scene_here = scene[t]
            bias = []
            for e in range(5):
                u = t + e - 2
                there = scene[jnp.clip(u, 0, 127)]
                inside = jnp.logical_and(u >= 0, u < 128)
                bias.append(jnp.where(jnp.logical_and(inside, there == scene_here), 0.0, -jnp.inf).astype(F32))
            turned = packed if parity == 0 else pltpu.roll(packed, 64, 1)
            query = jnp.where(low256, turned, 0.0).astype(BF16)
            scores = [dot_t(query, keys[parity + e]) for e in range(5)]
            tops = [jnp.maximum(one[:, :128], one[:, 128:]) + bias[e] for e, one in enumerate(scores)]
            top = jnp.max(functools.reduce(jnp.maximum, tops), axis=1, keepdims=True) * EXP_SCALE
            raised = [
                jnp.exp2((one * EXP_SCALE - (top - bias[e])).astype(BF16)) for e, one in enumerate(scores)
            ]
            both = dot(jnp.concatenate(raised, axis=1), jnp.concatenate(values[parity : parity + 5], axis=0))
            other_way = pltpu.roll(both, 64, 1)
            outs.append(other_way / both if parity == 0 else both / other_way)
        whole = jnp.where(low256, outs[0], outs[1])
        mixed[sh, :, k] = whole.astype(BF16).reshape(4, 4, 16, 128)

    def heads_own(sh, k):
        return pltpu.make_async_copy(mixed.at[sh, y, k], heads.at[sh, y, k], turn_s.at[sh, k])

    def send_heads(sh, k):
        for d in (2, 1, 3):
            t = (y + d) % 4
            remote(
                mixed.at[sh, t, k], heads.at[sh, y, k], h_s, h_r.at[sh, k], at(x, t, z, c)
            ).start()
        heads_own(sh, k).start()

    def normed_copy(sh, f):
        return remote(
            normed.at[f, sh], group.at[me, sh], n_s, n_r.at[sh, x], at(f // 2, y, z, f % 2)
        )

    def a_part(t, k):
        return remote(za.at[t, k], back_a.at[z, k], a_s, a_r, at(x, y, t, c))

    def project(sh, k):
        arrived(heads.at[sh, three, k], h_r.at[sh, k], buddy)
        heads_own(sh, k).wait()
        part = [heads[sh, h, k].reshape(64, 128).astype(F32) for h in range(HEADS)]
        mixes = []
        for parity in range(2):
            lanes = []
            for hp in range(2):
                first, second = part[2 * hp], part[2 * hp + 1]
                if parity == 0:
                    lanes.append(jnp.where(low64, first, pltpu.roll(second, 64, 1)))
                else:
                    lanes.append(jnp.where(low64, pltpu.roll(first, 64, 1), second))
            mixes.append(jnp.concatenate(lanes, axis=1))
        for sl in range(8):
            rows = slice(8 * sl, 8 * sl + 8)
            two = jnp.concatenate([mixes[0][rows], mixes[1][rows]], axis=0)
            za[8 * sh + sl, k] = two.astype(BF16)
        rows = jnp.concatenate(mixes, axis=0).astype(BF16)
        update = dot(rows, out_one[...])
        held = tok2[pl.ds(2 * k, 2), pl.ds(4 * sh, 4)].astype(F32)
        after = (held.reshape(2, 64, 512) + emb[...][None]).reshape(128, 512) + update
        normed[pl.ds(2 * k, 2), sh] = rms(after, gain_two[...]).reshape(2, 64, 512)

    def send_normed(sh, k):
        normed_copy(sh, 2 * k).start()
        normed_copy(sh, 2 * k + 1).start()

    def send_last(sh):
        normed_copy(sh, 2 * x + 1 - c).start()
        group[me, sh] = normed[me, sh]

    def send_a(sh, k):
        @pl.when(sh == zh)
        def _():
            back_a[z, k] = za[z, k]

        @pl.when(sh != zh)
        def _():
            a_part(8 * sh + zl, k).start()

        def send(i, carry):
            a_part(8 * sh + (zl + i) % 8, k).start()
            return carry

        lax.fori_loop(1, 8, send, 0)

    for sh in range(2):
        all_here(sh)
        edge_here(0, sh)
        edge_here(1, sh)

    def unit(i, carry):
        k = (x + 1 + i // 2) % 4
        sh = (zh + i) % 2
        attend(sh, k)
        send_heads(sh, k)

        @pl.when(i > 1)
        def _():
            done = (x + i // 2) % 4
            project(sh, done)
            send_normed(sh, done)
            send_a(sh, done)

        return carry

    lax.fori_loop(0, 8, unit, 0)

    def last_unit(i, carry):
        sh = (zh + i) % 2
        project(sh, x)
        send_last(sh)
        send_a(sh, x)
        return carry

    lax.fori_loop(0, 2, last_unit, 0)

    def qkv(xs, sh):
        rows = group[pl.ds(2 * xs, 2), sh].reshape(128, 512)
        query = dot(rows, wq2[...]).astype(BF16).reshape(2, 4, 16, 256)
        key = (dot(rows, wk2[...]) * key_gain_two[...]).astype(BF16).reshape(2, 4, 16, 256)
        value = dot(rows, wv2[...]).astype(BF16).reshape(2, 4, 16, 256)
        for core in range(2):
            q2[:, 4 * xs + 2 * core + sh] = query[core]
            k2[:, 4 * xs + 2 * core + sh] = key[core]
            v2[:, 4 * xs + 2 * core + sh] = value[core]

    def all_qkv(sh):
        arrived(group.at[2 * x + 1 - c, sh], n_r.at[sh, x], buddy)
        qkv(x, sh)

        def next_x(i, carry):
            xs = (x + i) % 4
            arrived(group.at[pl.ds(2 * xs, 2), sh], n_r.at[sh, xs], buddy)
            qkv(xs, sh)
            return carry

        lax.fori_loop(1, 4, next_x, 0)

    all_qkv(zh)
    all_qkv(1 - zh)

    row = lax.broadcasted_iota(jnp.int32, (256, 256), 0) % 16
    column = lax.broadcasted_iota(jnp.int32, (256, 256), 1)
    alike = row == column % 16
    head_of = column // HEAD_DIM

    def cross(g):
        query = q2[g].reshape(256, 256)
        key = k2[g].reshape(256, 256)
        value = v2[g].reshape(256, 256)
        result = jnp.zeros((256, 256), F32)
        for h in range(HEADS):
            mine = head_of == h
            one = jnp.where(mine, query.astype(F32), 0.0).astype(BF16)
            scores = jnp.where(alike, dot_t(one, key), -jnp.inf)
            top = jnp.max(scores, axis=1, keepdims=True)
            raised = jnp.exp2((scores - top) * EXP_SCALE)
            total = jnp.sum(raised, axis=1, keepdims=True)
            result = jnp.where(mine, dot(raised.astype(BF16), value) / total, result)
        crossed[g] = result.astype(BF16).reshape(8, 2, 16, 256)

    def b_copy(t):
        return remote(zb.at[t], back_b.at[z], b_s, b_r, at(x, y, t, c))

    def send_crossed(g):
        def send(i, carry):
            s = (me + i) % 8
            remote(
                crossed.at[g, s], returned.at[g, me], x_s, x_r.at[g], at(s // 2, y, z, s % 2)
            ).start()
            return carry

        lax.fori_loop(1, 8, send, 0)
        returned[g, me] = crossed[g, me]

    def send_b(g):
        arrived(returned.at[g, seven], x_r.at[g], buddy)
        for sh in range(2):
            block = returned[g, :, sh].astype(F32)
            for parity in range(2):
                rows = slice(8 * parity, 8 * parity + 8)
                whole = jnp.concatenate([block[f, rows] for f in range(8)], axis=0)
                t = 8 * sh + 2 * g + parity
                zb[t] = whole.astype(BF16).reshape(4, 16, 256)

                @pl.when(t != z)
                def _(t=t):
                    b_copy(t).start()

    def one_group(i, carry):
        g = (z // 2 + i) % 4
        cross(g)
        send_crossed(g)

        @pl.when(i > 0)
        def _():
            send_b((z // 2 + i + 3) % 4)

        return carry

    lax.fori_loop(0, 4, one_group, 0)
    send_b((z // 2 + 3) % 4)
    back_b[z] = zb[z]

    sent(land.at[fifteen], tok_s, buddy)
    sent(kv_out.at[three], kv_s, buddy)
    sent(q_out.at[three], q_s, buddy)
    sent(kv_out.at[:, :, pl.ds(0, 4)], edge_s, buddy)
    sent(mixed.at[:, three], h_s, buddy)
    sent(normed.at[seven], n_s, buddy)
    sent(crossed.at[:, seven], x_s, buddy)
    sent(za.at[fifteen], a_s, buddy)
    sent(zb.at[fifteen], b_s, buddy)
    arrived(back_a.at[fifteen], a_r, buddy)
    arrived(back_b.at[fifteen], b_r, buddy)


def final_kernel(ids, tok, table, back_a, back_b, out_one, out_two, out, emb):
    @pl.when(pl.program_id(0) == 0)
    def _():
        emb[...] = one_hot_rows(id_rows(ids), table[...])

    mixed_a = back_a[...].reshape(512, 256)
    mixed_b = back_b[...].reshape(512, 256)
    update = dot(mixed_a, out_one[...]) + dot(mixed_b, out_two[...])
    rows = tok[...].astype(F32) + emb[...][:, None]
    out[...] = rows + jnp.transpose(update.reshape(64, 8, 512), (1, 0, 2))


VMEM = pl.BlockSpec(memory_space=pltpu.VMEM)
SMEM = pl.BlockSpec(memory_space=pltpu.SMEM)
DMA = pltpu.SemaphoreType.DMA


def shape(*dims, dtype=BF16):
    return jax.ShapeDtypeStruct(dims, dtype)


def params(**more):
    return pltpu.CompilerParams(vmem_limit_bytes=60 << 20, **more)


def on_device(
    tokens, patch_ids, patch_embed, scene_ids,
    norm_one, query_one, key_one, value_one, key_gain_one, out_one,
    norm_two, query_two, key_two, value_two, key_gain_two, out_two,
):
    tok = tokens.reshape(8, 16, 8, 512)
    back_a, back_b = pl.pallas_call(
        layer_kernel,
        out_shape=(shape(16, 4, 16, 256), shape(16, 4, 16, 256)),
        in_specs=[SMEM, SMEM, pl.BlockSpec(memory_space=pl.ANY)] + [VMEM] * 12,
        out_specs=(VMEM,) * 2,
        scratch_shapes=[
            pltpu.VMEM((16, 8, 8, 512), BF16),
            pltpu.VMEM((8, 8, 128), jnp.int32),
            pltpu.VMEM((64, 512), F32),
            pltpu.VMEM((8, 8, 16, 512), BF16),
            pltpu.VMEM((4, 8, 4, 16, 128), BF16),
            pltpu.VMEM((4, 8, 8, 16, 128), BF16),
            pltpu.VMEM((4, 8, 4, 16, 128), BF16),
            pltpu.VMEM((4, 8, 12, 16, 128), BF16),
            pltpu.VMEM((2, 4, 4, 4, 16, 128), BF16),
            pltpu.VMEM((2, 4, 4, 4, 16, 128), BF16),
            pltpu.VMEM((16, 4, 16, 256), BF16),
            pltpu.VMEM((16, 4, 16, 256), BF16),
            pltpu.VMEM((8, 2, 64, 512), BF16),
            pltpu.VMEM((8, 2, 64, 512), BF16),
            pltpu.VMEM((4, 16, 16, 256), BF16),
            pltpu.VMEM((4, 16, 16, 256), BF16),
            pltpu.VMEM((4, 16, 16, 256), BF16),
            pltpu.VMEM((4, 8, 2, 16, 256), BF16),
            pltpu.VMEM((4, 8, 2, 16, 256), BF16),
            DMA, DMA((8,)), DMA, DMA, DMA, DMA((2,)), DMA, DMA((2,)), DMA((2, 2)), DMA, DMA((2, 2)),
            DMA, DMA((2, 4)), DMA, DMA((2, 4)), DMA, DMA((4,)),
            DMA, DMA, DMA, DMA, DMA((2, 4)), DMA,
        ],
        compiler_params=params(collective_id=0, has_side_effects=True),
        name="layer",
    )(
        scene_ids, patch_ids, tok, patch_embed, norm_one[None], query_one, key_one, value_one, key_gain_one[None],
        out_one, norm_two[None], query_two, key_two, value_two, key_gain_two[None],
    )
    out = pl.pallas_call(
        final_kernel,
        grid=(2,),
        out_shape=shape(8, 128, 512, dtype=F32),
        in_specs=[
            SMEM,
            pl.BlockSpec((8, 64, 512), lambda i: (0, i, 0)),
            VMEM,
            pl.BlockSpec((8, 4, 16, 256), lambda i: (i, 0, 0, 0)),
            pl.BlockSpec((8, 4, 16, 256), lambda i: (i, 0, 0, 0)),
            VMEM,
            VMEM,
        ],
        out_specs=pl.BlockSpec((8, 64, 512), lambda i: (0, i, 0)),
        scratch_shapes=[pltpu.VMEM((8, 512), F32)],
        compiler_params=params(),
        name="final",
    )(patch_ids, tokens[0], patch_embed, back_a, back_b, out_one, out_two)
    return out.reshape(1, 8, 128, 512)


def solution(mesh):
    return jax.shard_map(
        on_device,
        mesh=mesh,
        in_specs=(P("subj", "patch", None, None), P("patch")) + (P(),) * 14,
        out_specs=P("subj", "patch", None, None),
        check_vma=False,
    )
```
